256 devices in a mesh: recv: 64 (over y, x, z_hi), seg: 4 (over z_lo, core).
Axes of the slice: x: 4, y: 4, z: 8 (z_hi: 4, z_lo: 2; z = z_hi * 2 + z_lo), core: 2. Of those that a mesh axis runs over, the one named last changes fastest.
Arguments:
- raw_data: float32 [8, 4096, 2048], P('seg', 'recv'), may hold values from -210 to 210
- row_owner: int32 [4096, 1], P('recv'), may hold values from 0 to 63; in each aligned block of 64 rows (0 to 63, 64 to 127, ...) at most 2 rows name the same one
- source_blocks: int32 [2], replicated, may hold values from 0 to 63, as said below
Outputs:
- correlations: bfloat16 [2, 128, 8192, 512], P(None, 'seg', 'recv')
The draws below stay inside these ranges and needn't reach their ends.
Inputs may be any that keep to these rules, and one draw needn't show every extreme that they name: `row_owner`: within the rows of one device (aligned blocks of 64 rows) no owner is named by more than 2 rows, a bound that some block reaches. `source_blocks`: the ids are distinct, and one of them is always the last block; block b covers channel slots b * 128 to (b + 1) * 128 - 1.
All inputs are finite; a program needn't handle non-finite values. Where the reference program divides by a largest or mean magnitude, that divisor is 1e-20 or more.
Results may differ from the reference program's by a relative error of at most 0.0068.
Values may be sent and summed in bfloat16 or wider, within the bound.
A program may use at most 128 MiB of HBM per device.

```python
import math
import jax
import jax.numpy as jnp
import numpy as np
from jax import lax

WIN = 512
NB = 128
SRC_W = 128
SRC_BLK = 2
WINS = 4
RAW_DEV = 64
CAP = 2
RCV_SLOTS = 128
RAW_ROWS = 4096
CHANNELS = 8192
SEGMENTS = 8
SAMP = 2048
N_RECV = 64


def draw_raw_data(key, part):
    key_base, key_scale = jax.random.split(key, 2)
    block_count = SAMP // NB
    base = jnp.clip(jax.random.normal(key_base, (SEGMENTS, RAW_ROWS, block_count, NB), jnp.float32), -5.0, 5.0)
    scales = jnp.exp(jax.random.uniform(key_scale, (SEGMENTS, RAW_ROWS, block_count, 1), jnp.float32, 0.0, math.log(10.0)))
    values = base * scales
    return values.reshape(SEGMENTS, RAW_ROWS, SAMP)


def draw_source_blocks(key, part):
    key_order, key_place = jax.random.split(jax.random.fold_in(key, 17), 2)
    block_total = CHANNELS // SRC_W
    ordering = jax.random.permutation(key_order, block_total - 1)[:SRC_BLK].astype(jnp.int32)
    position = jax.random.randint(key_place, (), 0, SRC_BLK).astype(jnp.int32)
    places = jnp.arange(SRC_BLK, dtype=jnp.int32)
    return jnp.where(places == position, jnp.int32(block_total - 1), ordering).astype(jnp.int32)


def deal_out(stream_key, own, number, rows, number_of, top, most, skew):
    sequence = jax.random.permutation(stream_key, number_of)
    heavy_load, usual = shares(number_of, rows * top, most, skew, True), shares(number_of, rows * top, most, skew, False)
    places = jnp.arange(number_of)

    def named(lengths, rotation):
        used = int((lengths > 0).sum())
        fixed = max(1, used // 4)
        shifted = fixed + (places - fixed + rotation * (used - fixed)) % max(1, number_of - fixed)
        return jnp.zeros((number_of,), jnp.int32).at[sequence[jnp.where(places < fixed, places, shifted)]].set(jnp.asarray(lengths, jnp.int32))

    lengths = jnp.where(number % 4 == 0, named(heavy_load, number // 4), named(usual, number - number // 4 - 1))
    mixed = jax.random.permutation(jax.random.fold_in(own, 3), number_of)
    donor, sink = mixed[0:number_of // 2 * 2:2], mixed[1:number_of // 2 * 2:2]
    margin = jnp.minimum(lengths[donor] - 1, most - lengths[sink]) // 2
    margin = jnp.where((donor == sequence[0]) | (sink == sequence[0]) | (lengths[sink] == 0), 0, jnp.maximum(margin, 0))
    shifted = jax.random.randint(jax.random.fold_in(own, 4), (number_of // 2,), 0, 1 << 20) % (margin + 1)
    lengths = lengths.at[donor].add(-shifted).at[sink].add(shifted)
    items = jnp.searchsorted(jnp.cumsum(lengths), jnp.arange(rows * top), side="right").astype(jnp.int32)
    grid = items.reshape(top, rows).T
    grid = grid[jax.random.permutation(jax.random.fold_in(own, 1), rows)]
    rotation = jax.random.randint(jax.random.fold_in(own, 2), (rows, 1), 0, top)
    return jnp.take_along_axis(grid, (jnp.arange(top)[None, :] + rotation) % top, axis=1)


def shares(amount, total, limit, slope, full):
    loads = [(1 << 20) // math.isqrt(standing ** slope) + 1 for standing in range(1, amount + 1)]
    largest = limit if full else min(limit, max(-(-total // amount), total * loads[0] // sum(loads)))
    least = 1 if total - largest >= amount - 1 else 0
    counts, rest = [largest] + [least] * (amount - 1), total - largest - least * (amount - 1)
    while rest > 0:
        movable = [i for i in range(1, amount) if counts[i] < largest] or [i for i in range(1, amount) if counts[i] < limit]
        mass, remaining = sum([loads[i] for i in movable]), rest
        for i in movable:
            extra = min(limit - counts[i], max(1, remaining * loads[i] // mass), rest)
            counts[i] = counts[i] + extra
            rest = rest - extra
    return np.array(counts)


def setup_inputs(seed: int = 0) -> dict:
    key_of = jax.random.split(jax.random.key(seed), 4)
    raw_data = draw_raw_data(jax.random.fold_in(key_of[3], 71), 0)
    row_owner_keys = jax.random.split(jax.random.fold_in(key_of[1], 1), RAW_ROWS // RAW_DEV)
    row_owner_turns = jax.random.permutation(jax.random.fold_in(key_of[1], 3), RAW_ROWS // RAW_DEV)
    row_owner = jax.vmap(lambda own, number: deal_out(jax.random.fold_in(key_of[1], 2), own, number, RAW_DEV, N_RECV, 1, CAP, 2))(row_owner_keys, row_owner_turns).reshape((RAW_ROWS, 1))
    source_blocks = draw_source_blocks(jax.random.fold_in(key_of[3], 71), 0)
    return {"raw_data": raw_data, "row_owner": row_owner, "source_blocks": source_blocks}


def forward_table(length):
    half_win = length // 2
    sample_ids = jnp.arange(length, dtype=jnp.int32)
    freq_ids = jnp.arange(half_win, dtype=jnp.int32)
    angles = (sample_ids[:, None] * freq_ids[None, :] % length).astype(jnp.float32) * (2.0 * math.pi / length)
    parity = jnp.where(sample_ids % 2 == 0, 1.0, -1.0).astype(jnp.float32)
    sines = jnp.where(freq_ids[None, :] == 0, parity[:, None], -jnp.sin(angles))
    return jnp.concatenate([jnp.cos(angles), sines], axis=1)

def inverse_table(length, window_total):
    half_win = length // 2
    lag_ids = jnp.arange(length, dtype=jnp.int32) - half_win
    freq_ids = jnp.arange(half_win, dtype=jnp.int32)
    angles = (freq_ids[:, None] * lag_ids[None, :] % length).astype(jnp.float32) * (2.0 * math.pi / length)
    factor = 1.0 / (length * math.sqrt(window_total * length))
    parity = jnp.where(lag_ids % 2 == 0, 1.0, -1.0).astype(jnp.float32)
    first = freq_ids[:, None] == 0
    cosine_rows = jnp.where(first, factor * jnp.ones_like(angles), 2.0 * factor * jnp.cos(angles))
    sine_rows = jnp.where(first, factor * parity[None, :] * jnp.ones_like(angles), -2.0 * factor * jnp.sin(angles))
    return jnp.concatenate([cosine_rows, sine_rows], axis=0).astype(jnp.bfloat16)

def normalize(series):
    blocks = series.reshape(series.shape[:-1] + (series.shape[-1] // NB, NB))
    amplitude = lax.optimization_barrier(jnp.mean(jnp.abs(blocks), axis=-1, keepdims=True)) + 1e-06
    return (blocks / amplitude).reshape(series.shape)

def spectra_of(series, dft_table):
    row_count = series.shape[0]
    windows = normalize(series).reshape(row_count, -1, dft_table.shape[0])
    return jnp.einsum('nkt,tj->nkj', windows, dft_table, precision=lax.Precision.HIGHEST).astype(jnp.bfloat16)

def cross_terms(source, receiver):
    half_win = source.shape[-1] // 2
    swapped = jnp.concatenate([receiver[..., half_win:], receiver[..., :half_win]], axis=-1)
    direct = jnp.einsum('skf,rkf->srf', source, receiver, precision=lax.Precision.HIGHEST)
    crossed = jnp.einsum('skf,rkf->srf', source, swapped, precision=lax.Precision.HIGHEST)
    interior = (jnp.arange(half_win) > 0).astype(direct.dtype)
    real_part = direct[..., :half_win] + interior * direct[..., half_win:]
    imag_part = interior * (crossed[..., :half_win] - crossed[..., half_win:]) + (1.0 - interior) * direct[..., half_win:]
    return jnp.concatenate([real_part, imag_part], axis=-1)

def reference(raw_data, row_owner, source_blocks):
    forward = forward_table(WIN)
    rows_first = jnp.transpose(raw_data, (1, 0, 2))
    row_spectra = spectra_of(rows_first, forward)
    owners = row_owner[:, 0].reshape(N_RECV, RAW_DEV)
    onehot = (owners[:, :, None] == jnp.arange(N_RECV, dtype=jnp.int32)[None, None, :]).astype(jnp.int32)
    rank_in_owner = lax.optimization_barrier(jnp.sum(onehot * (jnp.cumsum(onehot, axis=1) - 1), axis=2))
    senders = jnp.arange(N_RECV, dtype=jnp.int32)[:, None]
    slot_index = (owners * RCV_SLOTS + senders * CAP + rank_in_owner).reshape(-1).astype(jnp.int32)
    channel_spectra = jnp.zeros((CHANNELS, SEGMENTS * WINS, WIN), jnp.bfloat16).at[slot_index].set(row_spectra)
    source_rows = (source_blocks[:, None] * SRC_W + jnp.arange(SRC_W, dtype=jnp.int32)[None, :]).reshape(-1)
    sources = channel_spectra[source_rows].astype(jnp.float32)
    inverse = inverse_table(WIN, SEGMENTS * WINS).astype(jnp.float32)

    def owner_block(owner_id):
        receivers = lax.dynamic_slice_in_dim(channel_spectra, (owner_id * RCV_SLOTS).astype(jnp.int32), RCV_SLOTS, 0).astype(jnp.float32)
        stacked = lax.optimization_barrier(cross_terms(sources, receivers).astype(jnp.bfloat16)).astype(jnp.float32)
        lagged = jnp.einsum('srf,fl->srl', stacked, inverse, precision=lax.Precision.HIGHEST)
        return lagged.astype(jnp.bfloat16)
    blocks = lax.map(owner_block, jnp.arange(N_RECV, dtype=jnp.int32))
    merged = jnp.transpose(blocks, (1, 0, 2, 3)).reshape(SRC_BLK, SRC_W, CHANNELS, WIN)
    return merged
```

```python
import math

import jax
import jax.numpy as jnp
from jax import lax
from jax.sharding import PartitionSpec as P

WIN = 512
NB = 128
SRC_W = 128


def forward_table(length):
    half_win = length // 2
    sample_ids = jnp.arange(length, dtype=jnp.int32)
    freq_ids = jnp.arange(half_win, dtype=jnp.int32)
    angles = (sample_ids[:, None] * freq_ids[None, :] % length).astype(jnp.float32) * (
        2.0 * math.pi / length
    )
    parity = jnp.where(sample_ids % 2 == 0, 1.0, -1.0).astype(jnp.float32)
    sines = jnp.where(freq_ids[None, :] == 0, parity[:, None], -jnp.sin(angles))
    return jnp.concatenate([jnp.cos(angles), sines], axis=1)


def inverse_table(length, window_total):
    half_win = length // 2
    lag_ids = jnp.arange(length, dtype=jnp.int32) - half_win
    freq_ids = jnp.arange(half_win, dtype=jnp.int32)
    angles = (freq_ids[:, None] * lag_ids[None, :] % length).astype(jnp.float32) * (
        2.0 * math.pi / length
    )
    factor = 1.0 / (length * math.sqrt(window_total * length))
    parity = jnp.where(lag_ids % 2 == 0, 1.0, -1.0).astype(jnp.float32)
    first = freq_ids[:, None] == 0
    cosine_rows = jnp.where(first, factor * jnp.ones_like(angles), 2.0 * factor * jnp.cos(angles))
    sine_rows = jnp.where(
        first, factor * parity[None, :] * jnp.ones_like(angles), -2.0 * factor * jnp.sin(angles)
    )
    return jnp.concatenate([cosine_rows, sine_rows], axis=0).astype(jnp.bfloat16)


def normalize(series):
    blocks = series.reshape(series.shape[:-1] + (series.shape[-1] // NB, NB))
    amplitude = jnp.mean(jnp.abs(blocks), axis=-1, keepdims=True) + 1e-06
    return (blocks / amplitude).reshape(series.shape)


def cross_terms(source, receiver):
    half_win = source.shape[-1] // 2
    swapped = jnp.concatenate([receiver[..., half_win:], receiver[..., :half_win]], axis=-1)
    direct = jnp.einsum("skf,rkf->srf", source, receiver, preferred_element_type=jnp.float32)
    crossed = jnp.einsum("skf,rkf->srf", source, swapped, preferred_element_type=jnp.float32)
    interior = (jnp.arange(half_win) > 0).astype(jnp.float32)
    real_part = direct[..., :half_win] + interior * direct[..., half_win:]
    imag_part = (
        interior * (crossed[..., :half_win] - crossed[..., half_win:])
        + (1.0 - interior) * direct[..., half_win:]
    )
    return jnp.concatenate([real_part, imag_part], axis=-1)


def local(raw_data, row_owner, source_blocks):
    recv_count = lax.axis_size("recv")
    seg_count = lax.axis_size("seg")
    rows = row_owner.shape[0]
    capacity = 2
    slot_count = recv_count * capacity
    owner_ids = row_owner[:, 0]
    row_ids = jnp.arange(rows, dtype=jnp.int32)
    same = (owner_ids[:, None] == owner_ids[None, :]) & (row_ids[None, :] < row_ids[:, None])
    rank_in_owner = jnp.sum(same.astype(jnp.int32), axis=1)
    slot_index = owner_ids * capacity + rank_in_owner
    onehot = (jnp.arange(slot_count, dtype=jnp.int32)[:, None] == slot_index[None, :]).astype(
        jnp.bfloat16
    )
    windows = normalize(raw_data).reshape(raw_data.shape[0], rows, -1, WIN)
    spectra = jnp.einsum(
        "snwt,tj->nswj", windows, forward_table(WIN), precision=lax.Precision.HIGHEST
    ).astype(jnp.bfloat16)
    spectra = spectra.reshape(rows, -1)
    slots = jnp.dot(onehot, spectra, preferred_element_type=jnp.float32).astype(jnp.bfloat16)
    slots = slots.reshape(recv_count, capacity, -1, WIN)
    wins = slots.shape[2]

    mine = jnp.stack(
        [lax.dynamic_index_in_dim(slots, source_blocks[b], 0, keepdims=False) for b in range(2)]
    )
    inner = recv_count // seg_count
    pairs = []
    for outer in range(seg_count):
        for r in range(inner):
            for k in range(seg_count):
                pairs.append(
                    (
                        (outer * inner + r) * seg_count + k,
                        (k * inner + r) * seg_count + outer,
                    )
                )
    mine = lax.ppermute(mine, ("recv", "seg"), pairs)
    panels = lax.all_gather(mine, "recv", axis=0, tiled=False)
    panels = panels.reshape(seg_count, inner, 2, capacity, wins, WIN)
    sources = jnp.transpose(panels, (2, 1, 3, 0, 4, 5)).reshape(
        2 * inner * capacity, seg_count * wins, WIN
    )

    held = lax.all_to_all(slots, "recv", split_axis=0, concat_axis=0, tiled=True)
    held = held.reshape(slot_count, wins, WIN)
    receivers = lax.all_gather(held, "seg", axis=1, tiled=True)
    stacked = cross_terms(sources, receivers).astype(jnp.bfloat16)
    inverse = inverse_table(WIN, seg_count * wins)
    lagged = jnp.dot(stacked.reshape(-1, WIN), inverse, preferred_element_type=jnp.float32)
    return lagged.astype(jnp.bfloat16).reshape(2, SRC_W // seg_count, slot_count, WIN)


def solution(mesh):
    placed = (P("seg", "recv", None), P("recv", None), P())
    return jax.shard_map(
        local, mesh=mesh, in_specs=placed, out_specs=P(None, "seg", "recv", None), check_vma=False
    )
```

```python
import math

import jax
import jax.numpy as jnp
from jax import lax
from jax.experimental import pallas as pl
from jax.experimental.pallas import tpu as pltpu
from jax.sharding import PartitionSpec as P

WIN = 512
NB = 128
SRC_W = 128


def forward_table(length):
    half_win = length // 2
    sample_ids = jnp.arange(length, dtype=jnp.int32)
    freq_ids = jnp.arange(half_win, dtype=jnp.int32)
    angles = (sample_ids[:, None] * freq_ids[None, :] % length).astype(jnp.float32) * (
        2.0 * math.pi / length
    )
    parity = jnp.where(sample_ids % 2 == 0, 1.0, -1.0).astype(jnp.float32)
    sines = jnp.where(freq_ids[None, :] == 0, parity[:, None], -jnp.sin(angles))
    return jnp.concatenate([jnp.cos(angles), sines], axis=1)


def inverse_table(length, window_total):
    half_win = length // 2
    lag_ids = jnp.arange(length, dtype=jnp.int32) - half_win
    freq_ids = jnp.arange(half_win, dtype=jnp.int32)
    angles = (freq_ids[:, None] * lag_ids[None, :] % length).astype(jnp.float32) * (
        2.0 * math.pi / length
    )
    factor = 1.0 / (length * math.sqrt(window_total * length))
    parity = jnp.where(lag_ids % 2 == 0, 1.0, -1.0).astype(jnp.float32)
    first = freq_ids[:, None] == 0
    cosine_rows = jnp.where(first, factor * jnp.ones_like(angles), 2.0 * factor * jnp.cos(angles))
    sine_rows = jnp.where(
        first, factor * parity[None, :] * jnp.ones_like(angles), -2.0 * factor * jnp.sin(angles)
    )
    return jnp.concatenate([cosine_rows, sine_rows], axis=0).astype(jnp.bfloat16)


def normalize(series):
    blocks = series.reshape(series.shape[:-1] + (series.shape[-1] // NB, NB))
    amplitude = jnp.mean(jnp.abs(blocks), axis=-1, keepdims=True) + 1e-06
    return (blocks / amplitude).reshape(series.shape)


def cross_terms(source, receiver):
    half_win = source.shape[-1] // 2
    swapped = jnp.concatenate([receiver[..., half_win:], receiver[..., :half_win]], axis=-1)
    direct = jnp.einsum("skf,rkf->srf", source, receiver, preferred_element_type=jnp.float32)
    crossed = jnp.einsum("skf,rkf->srf", source, swapped, preferred_element_type=jnp.float32)
    interior = (jnp.arange(half_win) > 0).astype(jnp.float32)
    real_part = direct[..., :half_win] + interior * direct[..., half_win:]
    imag_part = (
        interior * (crossed[..., :half_win] - crossed[..., half_win:])
        + (1.0 - interior) * direct[..., half_win:]
    )
    return jnp.concatenate([real_part, imag_part], axis=-1)


MESH = pl.DeviceIdType.MESH
ORDER = (2, 1, 3, 0)


def exchange_kernel(slots, chunk, held, panels, staged, xy_send, xy_recv, z_send, z_recv,
                    core_send, core_recv, pz_send, pz_recv, pxy_send, pxy_recv, local_sem):
    recv = lax.axis_index("recv")
    seg = lax.axis_index("seg")
    y, x, zh = recv // 16, (recv // 4) % 4, recv % 4
    zl, core = seg // 2, seg % 2
    plane = y * 4 + x

    def plane_peer(step):
        return ((y + step // 4) % 4) * 4 + (x + step % 4) % 4

    def xy_copy(turn, step):
        target = plane_peer(step)
        block = (zh + turn) % 4
        return pltpu.make_async_remote_copy(
            src_ref=slots.at[target, block],
            dst_ref=staged.at[block, plane],
            send_sem=xy_send.at[turn, step],
            recv_sem=xy_recv.at[turn, step],
            device_id=(target * 4 + zh, seg),
            device_id_type=MESH,
        )

    def z_copy(turn, low):
        block = (zh + turn) % 4
        return pltpu.make_async_remote_copy(
            src_ref=staged.at[block],
            dst_ref=held.at[(zh * 2 + zl) * 2 + core],
            send_sem=z_send.at[turn, low],
            recv_sem=z_recv.at[turn, zl],
            device_id=(plane * 4 + block, low * 2 + core),
            device_id_type=MESH,
        )

    def z_arrival(turn, low):
        place = (((zh + 4 - turn) % 4) * 2 + low) * 2 + core
        return pltpu.make_async_remote_copy(
            src_ref=staged.at[0],
            dst_ref=held.at[place],
            send_sem=z_send.at[turn, low],
            recv_sem=z_recv.at[turn, low],
            device_id=(recv, seg),
            device_id_type=MESH,
        )

    def core_copy(turn, low):
        place = (((zh + 4 - turn) % 4) * 2 + low) * 2 + core
        return pltpu.make_async_remote_copy(
            src_ref=held.at[place],
            dst_ref=held.at[place],
            send_sem=core_send.at[turn, low],
            recv_sem=core_recv.at[turn, low],
            device_id=(recv, zl * 2 + 1 - core),
            device_id_type=MESH,
        )

    def pz_copy(turn):
        return pltpu.make_async_remote_copy(
            src_ref=chunk,
            dst_ref=panels.at[plane, zh],
            send_sem=pz_send.at[turn],
            recv_sem=pz_recv.at[turn],
            device_id=(plane * 4 + (zh + turn) % 4, seg),
            device_id_type=MESH,
        )

    def pxy_copy(step):
        return pltpu.make_async_remote_copy(
            src_ref=panels.at[plane],
            dst_ref=panels.at[plane],
            send_sem=pxy_send.at[step],
            recv_sem=pxy_recv.at[step],
            device_id=(plane_peer(step) * 4 + zh, seg),
            device_id_type=MESH,
        )

    barrier = pltpu.get_barrier_semaphore()

    @pl.loop(1, 16)
    def _(step):
        pl.semaphore_signal(barrier, inc=1, device_id=(plane_peer(step) * 4 + zh, seg), device_id_type=MESH)

    @pl.loop(1, 8)
    def _(step):
        z = (zh * 2 + zl + step) % 8
        pl.semaphore_signal(
            barrier, inc=1, device_id=(plane * 4 + z // 2, (z % 2) * 2 + core), device_id_type=MESH
        )

    pl.semaphore_signal(barrier, inc=1, device_id=(recv, zl * 2 + 1 - core), device_id_type=MESH)
    own_chunk = pltpu.make_async_copy(chunk, panels.at[plane, zh], local_sem.at[4])
    own_chunk.start()
    own = []
    for turn in ORDER:
        block = (zh + turn) % 4
        own.append(pltpu.make_async_copy(slots.at[plane, block], staged.at[block, plane], local_sem.at[turn]))
        own[-1].start()
    pl.semaphore_wait(barrier, 23)

    for turn in ORDER[:1]:
        @pl.loop(1, 16)
        def _(step):
            xy_copy(turn, step).start()
    for turn in (1, 2, 3):
        pz_copy(turn).start()
    for turn in ORDER[1:]:
        @pl.loop(1, 16)
        def _(step):
            xy_copy(turn, step).start()

    kept = None
    for number, turn in enumerate(ORDER):
        own[number].wait()

        @pl.loop(1, 16)
        def _(step):
            xy_copy(turn, step).wait_recv()

        if turn:
            z_copy(turn, 0).start()
            z_copy(turn, 1).start()
        else:
            z_copy(0, 1 - zl).start()
            kept = pltpu.make_async_copy(
                staged.at[zh], held.at[(zh * 2 + zl) * 2 + core], local_sem.at[5]
            )
            kept.start()
        if number == 0:
            own_chunk.wait()
            for other in (1, 2, 3):
                pz_copy(other).wait_recv()

            @pl.loop(1, 16)
            def _(step):
                pxy_copy(step).start()

    kept.wait()
    core_copy(0, zl).start()
    for turn in (1, 3, 2):
        for low in (0, 1):
            z_arrival(turn, low).wait_recv()
            core_copy(turn, low).start()
    z_arrival(0, 1 - zl).wait_recv()
    core_copy(0, 1 - zl).start()

    @pl.loop(1, 16)
    def _(step):
        pxy_copy(step).wait_recv()
        pxy_copy(step).wait_send()
        for turn in ORDER:
            xy_copy(turn, step).wait_send()

    for turn in (1, 2, 3):
        pz_copy(turn).wait_send()
        for low in (0, 1):
            z_copy(turn, low).wait_send()
    z_copy(0, 1 - zl).wait_send()
    for turn in range(4):
        for low in (0, 1):
            core_copy(turn, low).wait()


def exchange(slots, chunk):
    dma = pltpu.SemaphoreType.DMA
    rows, width = slots.shape[-2:]
    return pl.pallas_call(
        exchange_kernel,
        out_shape=(
            jax.ShapeDtypeStruct((16, 16, rows, width), jnp.bfloat16),
            jax.ShapeDtypeStruct((16, 4) + chunk.shape, jnp.bfloat16),
        ),
        in_specs=[pl.BlockSpec(memory_space=pltpu.VMEM)] * 2,
        out_specs=(pl.BlockSpec(memory_space=pltpu.VMEM),) * 2,
        scratch_shapes=[
            pltpu.VMEM((4, 16, rows, width), jnp.bfloat16),
            dma((4, 16)), dma((4, 16)), dma((4, 2)), dma((4, 2)), dma((4, 2)), dma((4, 2)),
            dma((4,)), dma((4,)), dma((16,)), dma((16,)), dma((6,)),
        ],
        compiler_params=pltpu.CompilerParams(
            collective_id=0, has_side_effects=True, vmem_limit_bytes=32 * 1024 * 1024
        ),
        name="exchange",
    )(slots, chunk)


def local(raw_data, row_owner, source_blocks):
    recv_count = lax.axis_size("recv")
    seg_count = lax.axis_size("seg")
    rows = row_owner.shape[0]
    capacity = 2
    slot_count = recv_count * capacity
    owner_ids = row_owner[:, 0]
    row_ids = jnp.arange(rows, dtype=jnp.int32)
    same = (owner_ids[:, None] == owner_ids[None, :]) & (row_ids[None, :] < row_ids[:, None])
    rank_in_owner = jnp.sum(same.astype(jnp.int32), axis=1)
    slot_index = owner_ids * capacity + rank_in_owner
    onehot = (jnp.arange(slot_count, dtype=jnp.int32)[:, None] == slot_index[None, :]).astype(
        jnp.bfloat16
    )
    windows = normalize(raw_data).reshape(raw_data.shape[0], rows, -1, WIN)
    spectra = jnp.einsum(
        "snwt,tj->nswj", windows, forward_table(WIN), precision=lax.Precision.HIGHEST
    ).astype(jnp.bfloat16)
    spectra = spectra.reshape(rows, -1)
    slots = jnp.dot(onehot, spectra, preferred_element_type=jnp.float32).astype(jnp.bfloat16)
    slots = slots.reshape(recv_count, capacity, -1, WIN)
    wins = slots.shape[2]

    mine = jnp.stack(
        [lax.dynamic_index_in_dim(slots, source_blocks[b], 0, keepdims=False) for b in range(2)]
    )
    inner = recv_count // seg_count
    pairs = []
    for outer in range(seg_count):
        for r in range(inner):
            for k in range(seg_count):
                pairs.append(
                    (
                        (outer * inner + r) * seg_count + k,
                        (k * inner + r) * seg_count + outer,
                    )
                )
    mine = lax.ppermute(mine, ("recv", "seg"), pairs)
    held, panels = exchange(
        slots.reshape(inner, seg_count, capacity * wins, WIN), mine.reshape(2 * capacity * wins, WIN)
    )
    panels = panels.reshape(seg_count, inner, 2, capacity, wins, WIN)
    sources = jnp.transpose(panels, (2, 1, 3, 0, 4, 5)).reshape(
        2 * inner * capacity, seg_count * wins, WIN
    )
    held = held.reshape(4, seg_count, inner, capacity, wins, WIN)
    receivers = jnp.transpose(held, (2, 0, 3, 1, 4, 5)).reshape(slot_count, seg_count * wins, WIN)
    stacked = cross_terms(sources, receivers).astype(jnp.bfloat16)
    inverse = inverse_table(WIN, seg_count * wins)
    lagged = jnp.dot(stacked.reshape(-1, WIN), inverse, preferred_element_type=jnp.float32)
    return lagged.astype(jnp.bfloat16).reshape(2, SRC_W // seg_count, slot_count, WIN)


def solution(mesh):
    placed = (P("seg", "recv", None), P("recv", None), P())
    return jax.shard_map(
        local, mesh=mesh, in_specs=placed, out_specs=P(None, "seg", "recv", None), check_vma=False
    )
```

```python
import functools
import math

import jax
import jax.numpy as jnp
import numpy as np
from jax import lax
from jax.experimental import pallas as pl
from jax.experimental.pallas import tpu as pltpu
from jax.sharding import PartitionSpec as P

WIN = 512
NB = 128
HALF = 256


def forward_table():
    sample, freq = np.arange(WIN), np.arange(HALF)
    angles = (sample[:, None] * freq[None, :] % WIN) * (2.0 * math.pi / WIN)
    parity = np.where(sample % 2 == 0, 1.0, -1.0)
    sines = np.where(freq[None, :] == 0, parity[:, None], -np.sin(angles))
    return np.concatenate([np.cos(angles), sines], axis=1)


def inverse_table(window_total):
    lag, freq = np.arange(WIN) - HALF, np.arange(HALF)
    angles = (freq[:, None] * lag[None, :] % WIN) * (2.0 * math.pi / WIN)
    factor = 1.0 / (WIN * math.sqrt(window_total * WIN))
    parity = np.where(lag % 2 == 0, 1.0, -1.0)
    zero = freq[:, None] == 0
    cosine_rows = np.where(zero, factor, 2.0 * factor * np.cos(angles))
    sine_rows = np.where(zero, factor * parity[None, :], -2.0 * factor * np.sin(angles))
    return np.concatenate([cosine_rows, sine_rows], axis=0)


def prepare_kernel(blocks, raw, owner_column, owner_row, slots, chunk, flat):
    row = lax.broadcasted_iota(jnp.int32, (64, 512), 0)
    lane = lax.broadcasted_iota(jnp.int32, (64, 512), 1)
    same = (owner_column[...] == owner_row[...]) & (row < lane % 64)
    rank = jnp.sum(same.astype(jnp.int32), axis=0, keepdims=True)
    target = (owner_row[...] * 2 + rank) * 8 + lax.broadcasted_iota(jnp.int32, (1, 512), 1) // 64
    for n in range(2):
        for run in range(16):
            values = raw[n, :, run * NB : (run + 1) * NB]
            amplitude = jnp.mean(jnp.abs(values), axis=-1, keepdims=True) + 1e-06
            place = n * 4 + run // 4
            flat[place * 64 : place * 64 + 64, run % 4 * NB : run % 4 * NB + NB] = (
                values / amplitude
            ).astype(jnp.bfloat16)

    @pl.loop(0, 4)
    def _(part):
        placed = lax.broadcasted_iota(jnp.int32, (256, 512), 0) + part * 256 == target
        slots[pl.ds(pl.multiple_of(part * 256, 256), 256), :] = jnp.dot(
            placed.astype(jnp.float32).astype(jnp.bfloat16), flat[...], preferred_element_type=jnp.float32
        ).astype(jnp.bfloat16)

    for b in range(2):
        chunk[b * 16 : b * 16 + 16, :] = slots[pl.ds(pl.multiple_of(blocks[b] * 16, 16), 16), :]


def prepare(raw_data, row_owner, source_blocks):
    vmem = pl.BlockSpec(memory_space=pltpu.VMEM)
    return pl.pallas_call(
        prepare_kernel,
        out_shape=(
            jax.ShapeDtypeStruct((1024, WIN), jnp.bfloat16),
            jax.ShapeDtypeStruct((32, WIN), jnp.bfloat16),
        ),
        in_specs=[pl.BlockSpec(memory_space=pltpu.SMEM), vmem, vmem, vmem],
        out_specs=(vmem, vmem),
        scratch_shapes=[pltpu.VMEM((512, WIN), jnp.bfloat16)],
        compiler_params=pltpu.CompilerParams(vmem_limit_bytes=24 * 1024 * 1024),
        name="prepare",
    )(source_blocks, raw_data, row_owner, jnp.tile(row_owner.reshape(1, 64), (1, 8)))


MESH = pl.DeviceIdType.MESH
ORDER = (2, 1, 3, 0)


def exchange_kernel(slots, first, held, panels, staged, chunk, turn_send, turn_recv, xy_send, xy_recv, z_send, z_recv,
                    core_send, core_recv, pz_send, pz_recv, pxy_send, pxy_recv, local_sem):
    recv = lax.axis_index("recv")
    seg = lax.axis_index("seg")
    y, x, zh = recv // 16, (recv // 4) % 4, recv % 4
    zl, core = seg // 2, seg % 2
    plane = y * 4 + x

    def plane_peer(step):
        return ((y + step // 4) % 4) * 4 + (x + step % 4) % 4

    def xy_copy(turn, step):
        target = plane_peer(step)
        block = (zh + turn) % 4
        return pltpu.make_async_remote_copy(
            src_ref=slots.at[target, block],
            dst_ref=staged.at[block, plane],
            send_sem=xy_send.at[turn, step],
            recv_sem=xy_recv.at[turn, step],
            device_id=(target * 4 + zh, seg),
            device_id_type=MESH,
        )

    def z_copy(turn, low):
        block = (zh + turn) % 4
        return pltpu.make_async_remote_copy(
            src_ref=staged.at[block],
            dst_ref=held.at[seg, :, zh],
            send_sem=z_send.at[turn, low],
            recv_sem=z_recv.at[turn, zl],
            device_id=(plane * 4 + block, low * 2 + core),
            device_id_type=MESH,
        )

    def z_arrival(turn, low):
        place = (zh + 4 - turn) % 4
        return pltpu.make_async_remote_copy(
            src_ref=staged.at[0],
            dst_ref=held.at[low * 2 + core, :, place],
            send_sem=z_send.at[turn, low],
            recv_sem=z_recv.at[turn, low],
            device_id=(recv, seg),
            device_id_type=MESH,
        )

    def core_copy(turn, low):
        place = (zh + 4 - turn) % 4
        return pltpu.make_async_remote_copy(
            src_ref=held.at[low * 2 + core, :, place],
            dst_ref=held.at[low * 2 + core, :, place],
            send_sem=core_send.at[turn, low],
            recv_sem=core_recv.at[turn, low],
            device_id=(recv, zl * 2 + 1 - core),
            device_id_type=MESH,
        )

    def pz_copy(turn):
        return pltpu.make_async_remote_copy(
            src_ref=chunk,
            dst_ref=panels.at[plane, zh],
            send_sem=pz_send.at[turn],
            recv_sem=pz_recv.at[turn],
            device_id=(plane * 4 + (zh + turn) % 4, seg),
            device_id_type=MESH,
        )

    def pxy_copy(step):
        return pltpu.make_async_remote_copy(
            src_ref=panels.at[plane],
            dst_ref=panels.at[plane],
            send_sem=pxy_send.at[step],
            recv_sem=pxy_recv.at[step],
            device_id=(plane_peer(step) * 4 + zh, seg),
            device_id_type=MESH,
        )

    def turn_copy():
        return pltpu.make_async_remote_copy(
            src_ref=first,
            dst_ref=chunk,
            send_sem=turn_send,
            recv_sem=turn_recv,
            device_id=((seg * 4 + x) * 4 + zh, y),
            device_id_type=MESH,
        )

    barrier = pltpu.get_barrier_semaphore()

    @pl.when(y != seg)
    def _():
        pl.semaphore_signal(barrier, inc=1, device_id=((seg * 4 + x) * 4 + zh, y), device_id_type=MESH)

    @pl.loop(1, 16)
    def _(step):
        pl.semaphore_signal(barrier, inc=1, device_id=(plane_peer(step) * 4 + zh, seg), device_id_type=MESH)

    @pl.loop(1, 8)
    def _(step):
        z = (zh * 2 + zl + step) % 8
        pl.semaphore_signal(
            barrier, inc=1, device_id=(plane * 4 + z // 2, (z % 2) * 2 + core), device_id_type=MESH
        )

    pl.semaphore_signal(barrier, inc=1, device_id=(recv, zl * 2 + 1 - core), device_id_type=MESH)
    kept_chunk = pltpu.make_async_copy(first, chunk, local_sem.at[6])
    own_chunk = pltpu.make_async_copy(chunk, panels.at[plane, zh], local_sem.at[4])

    @pl.when(y == seg)
    def _():
        kept_chunk.start()

    own = []
    for turn in ORDER:
        block = (zh + turn) % 4
        own.append(pltpu.make_async_copy(slots.at[plane, block], staged.at[block, plane], local_sem.at[turn]))
        own[-1].start()
    @pl.when(y == seg)
    def _():
        pl.semaphore_wait(barrier, 23)

    @pl.when(y != seg)
    def _():
        pl.semaphore_wait(barrier, 24)
        turn_copy().start()

    for turn in ORDER[:1]:
        @pl.loop(1, 16)
        def _(step):
            xy_copy(turn, step).start()
    for turn in ORDER[1:]:
        @pl.loop(1, 16)
        def _(step):
            xy_copy(turn, step).start()

    @pl.when(y != seg)
    def _():
        turn_copy().wait()

    @pl.when(y == seg)
    def _():
        kept_chunk.wait()

    own_chunk.start()
    for turn in (1, 2, 3):
        pz_copy(turn).start()

    kept = None
    for number, turn in enumerate(ORDER):
        own[number].wait()

        @pl.loop(1, 16)
        def _(step):
            xy_copy(turn, step).wait_recv()

        if turn:
            z_copy(turn, 0).start()
            z_copy(turn, 1).start()
        else:
            z_copy(0, 1 - zl).start()
            kept = pltpu.make_async_copy(
                staged.at[zh], held.at[seg, :, zh], local_sem.at[5]
            )
            kept.start()
        if number == 0:
            own_chunk.wait()
            for other in (1, 2, 3):
                pz_copy(other).wait_recv()

            @pl.loop(1, 16)
            def _(step):
                pxy_copy(step).start()

    kept.wait()
    core_copy(0, zl).start()
    for turn in (1, 3, 2):
        for low in (0, 1):
            z_arrival(turn, low).wait_recv()
            core_copy(turn, low).start()
    z_arrival(0, 1 - zl).wait_recv()
    core_copy(0, 1 - zl).start()

    @pl.loop(1, 16)
    def _(step):
        pxy_copy(step).wait_recv()
        pxy_copy(step).wait_send()
        for turn in ORDER:
            xy_copy(turn, step).wait_send()

    for turn in (1, 2, 3):
        pz_copy(turn).wait_send()
        for low in (0, 1):
            z_copy(turn, low).wait_send()
    z_copy(0, 1 - zl).wait_send()
    for turn in range(4):
        for low in (0, 1):
            core_copy(turn, low).wait()


def exchange(slots, chunk):
    dma = pltpu.SemaphoreType.DMA
    rows, width = slots.shape[-2:]
    return pl.pallas_call(
        exchange_kernel,
        out_shape=(
            jax.ShapeDtypeStruct((4, 16, 4, rows, width), jnp.bfloat16),
            jax.ShapeDtypeStruct((16, 4) + chunk.shape, jnp.bfloat16),
        ),
        in_specs=[pl.BlockSpec(memory_space=pltpu.VMEM)] * 2,
        out_specs=(pl.BlockSpec(memory_space=pltpu.VMEM),) * 2,
        scratch_shapes=[
            pltpu.VMEM((4, 16, rows, width), jnp.bfloat16),
            pltpu.VMEM(chunk.shape, jnp.bfloat16),
            dma, dma, dma((4, 16)), dma((4, 16)), dma((4, 2)), dma((4, 2)), dma((4, 2)), dma((4, 2)),
            dma((4,)), dma((4,)), dma((16,)), dma((16,)), dma((7,)),
        ],
        compiler_params=pltpu.CompilerParams(
            collective_id=0, has_side_effects=True, vmem_limit_bytes=32 * 1024 * 1024
        ),
        name="exchange",
    )(slots, chunk)


NT=(((1,),(1,)),((),())); TN=(((0,),(0,)),((),()))
def body(held, panels, fwd, inv, out, x, rf, lt, ss, *, per):
    f32=jnp.float32; bf=jnp.bfloat16
    @pl.when(pl.program_id(0)==0)
    def _():
        row=lax.broadcasted_iota(jnp.int32,(256,256),0); col=lax.broadcasted_iota(jnp.int32,(256,256),1)
        perm=((row%32)//2*16+row%2*8+row//32==col).astype(f32).astype(bf)
        @pl.loop(0,16)
        def _(n):
            k=n//4; g=n%4
            y=jnp.dot(perm, held[k,pl.ds(g*16,16)].reshape(256,512), preferred_element_type=f32).astype(bf)
            for w in range(8):
                x[pl.ds(pl.multiple_of((k*8+w)*128+g*32,32),32),:]=y[w*32:(w+1)*32]
        @pl.loop(0,16)
        def _(n):
            v=lax.dot_general(fwd[...], x[pl.ds(pl.multiple_of(n*256,256),256),:], NT, preferred_element_type=f32)
            for dw in range(2):
                for c in range(2):
                    rf[pl.ds(c*32+n*2+dw,256,stride=72),:]=v[c*256:(c+1)*256,dw*128:(dw+1)*128]
        perm2=((row%16)//2*32+(row%32)//16*16+row%2*8+row//32==col).astype(f32).astype(bf)
        @pl.loop(0,8)
        def _(n):
            k=n//2; g=n%2
            y=jnp.dot(perm2, panels[pl.ds(n*8,8)].reshape(256,512), preferred_element_type=f32).astype(bf)
            for w in range(8):
                for b in range(2):
                    for h in range(2):
                        x[pl.ds(pl.multiple_of((k*8+w)*128+h*64+b*32+g*16,16),16),:]=y[w*32+b*16:w*32+b*16+16]
        lane=lax.broadcasted_iota(jnp.int32,(256,128),1)<64
        first=lax.broadcasted_iota(jnp.int32,(256,128),0)==0
        @pl.loop(0,16)
        def _(n):
            v=lax.dot_general(fwd[...], x[pl.ds(pl.multiple_of(n*256,256),256),:], NT, preferred_element_type=f32)
            for dw in range(2):
                re=v[:256,dw*128:(dw+1)*128]; im=v[256:,dw*128:(dw+1)*128]
                lt[pl.ds(n*2+dw,256,stride=72),:]=jnp.where(lane,re,jnp.where(first,0.0,-im))
                lt[pl.ds(32+n*2+dw,256,stride=72),:]=jnp.where(lane,jnp.where(first,0.0,im),jnp.where(first,im,re))
        @pl.loop(0,256,unroll=8)
        def _(j):
            at=pl.ds(pl.multiple_of(j*72,8),64)
            s=lax.dot_general(lt[at,:].astype(bf), rf[at,:].astype(bf), TN, preferred_element_type=f32)
            ss[pl.ds(j,64,stride=520),:]=s[:64]
            ss[pl.ds(256+j,64,stride=520),:]=s[64:]
    base=pl.program_id(0)*per
    @pl.loop(0,per,unroll=4)
    def _(i):
        v=ss[pl.ds(pl.multiple_of((base+i)*520,8),512),:].astype(bf)
        out[i]=lax.dot_general(v, inv[...], TN, preferred_element_type=f32).astype(bf)

def compute(held, panels, fwd, inv, per=8):
    one=pl.Buffered(1)
    def whole(a): return pl.BlockSpec(a.shape, lambda i: (0,)*a.ndim, pipeline_mode=one)
    return pl.pallas_call(functools.partial(body,per=per), grid=(64//per,),
        out_shape=jax.ShapeDtypeStruct((64,128,512),jnp.bfloat16),
        in_specs=[whole(held),whole(panels),whole(fwd),whole(inv)],
        out_specs=pl.BlockSpec((per,128,512),lambda i:(i,0,0)),
        scratch_shapes=[pltpu.VMEM((4096,512),jnp.bfloat16),pltpu.VMEM((256*72,128),jnp.float32),
            pltpu.VMEM((256*72,128),jnp.float32),pltpu.VMEM((64*520,128),jnp.float32)],
        compiler_params=pltpu.CompilerParams(vmem_limit_bytes=56*1024*1024), name="correlate")(held,panels,fwd,inv)


def local(raw_data, row_owner, source_blocks):
    slots, chunk = prepare(raw_data, row_owner, source_blocks)
    held, panels = exchange(slots.reshape(16, 4, 16, WIN), chunk)
    forward = jnp.asarray(forward_table().T, jnp.bfloat16)
    inverse = jnp.asarray(inverse_table(32), jnp.bfloat16)
    lagged = compute(
        held.reshape(4, 64, 16, WIN), panels.reshape(64, 32, WIN), forward, inverse
    )
    return lagged.reshape(2, 32, 128, WIN)


def solution(mesh):
    placed = (P("seg", "recv", None), P("recv", None), P())
    return jax.shard_map(
        local, mesh=mesh, in_specs=placed, out_specs=P(None, "seg", "recv", None), check_vma=False
    )
```

```python
import functools
import math

import jax
import jax.numpy as jnp
import numpy as np
from jax import lax
from jax.experimental import pallas as pl
from jax.experimental.pallas import tpu as pltpu
from jax.sharding import PartitionSpec as P

WIN = 512
NB = 128
HALF = 256


def forward_table():
    sample, freq = np.arange(WIN), np.arange(HALF)
    angles = (sample[:, None] * freq[None, :] % WIN) * (2.0 * math.pi / WIN)
    parity = np.where(sample % 2 == 0, 1.0, -1.0)
    sines = np.where(freq[None, :] == 0, parity[:, None], -np.sin(angles))
    return np.concatenate([np.cos(angles), sines], axis=1)


def inverse_table(window_total):
    lag, freq = np.arange(WIN) - HALF, np.arange(HALF)
    angles = (freq[:, None] * lag[None, :] % WIN) * (2.0 * math.pi / WIN)
    factor = 1.0 / (WIN * math.sqrt(window_total * WIN))
    parity = np.where(lag % 2 == 0, 1.0, -1.0)
    zero = freq[:, None] == 0
    cosine_rows = np.where(zero, factor, 2.0 * factor * np.cos(angles))
    sine_rows = np.where(zero, factor * parity[None, :], -2.0 * factor * np.sin(angles))
    return np.concatenate([cosine_rows, sine_rows], axis=0)


def prepare_kernel(blocks, raw, owner, table, slots, chunk, spectra):
    row = lax.broadcasted_iota(jnp.int32, (64, 512), 0)
    lane = lax.broadcasted_iota(jnp.int32, (64, 512), 1)
    diagonal = row[:, :64] == lane[:, :64]
    owner_column = jnp.sum(jnp.where(diagonal, owner[...], 0), axis=1, keepdims=True)
    owner_row = jnp.sum(jnp.where(row == lane % 64, owner_column, 0), axis=0, keepdims=True)
    same = (owner_column == owner_row) & (row < lane % 64)
    rank = jnp.sum(same.astype(jnp.int32), axis=0, keepdims=True)
    target = (owner_row * 2 + rank) * 8 + lax.broadcasted_iota(jnp.int32, (1, 512), 1) // 64
    for window in range(8):
        parts = []
        for run in range(4):
            start = (window % 4 * 4 + run) * NB
            values = raw[window // 4, :, start : start + NB]
            amplitude = jnp.mean(jnp.abs(values), axis=-1, keepdims=True) + 1e-06
            parts.append(values / amplitude)
        spectra[window * 64 : window * 64 + 64, :] = jnp.dot(
            jnp.concatenate(parts, axis=1),
            table[...],
            precision=lax.Precision.HIGHEST,
            preferred_element_type=jnp.float32,
        ).astype(jnp.bfloat16)

    @pl.loop(0, 4)
    def _(part):
        placed = lax.broadcasted_iota(jnp.int32, (256, 512), 0) + part * 256 == target
        slots[pl.ds(pl.multiple_of(part * 256, 256), 256), :] = jnp.dot(
            placed.astype(jnp.float32).astype(jnp.bfloat16),
            spectra[...],
            preferred_element_type=jnp.float32,
        ).astype(jnp.bfloat16)

    for b in range(2):
        chunk[b * 16 : b * 16 + 16, :] = slots[pl.ds(pl.multiple_of(blocks[b] * 16, 16), 16), :]


def prepare(raw_data, row_owner, source_blocks):
    vmem = pl.BlockSpec(memory_space=pltpu.VMEM)
    return pl.pallas_call(
        prepare_kernel,
        out_shape=(
            jax.ShapeDtypeStruct((1024, WIN), jnp.bfloat16),
            jax.ShapeDtypeStruct((32, WIN), jnp.bfloat16),
        ),
        in_specs=[pl.BlockSpec(memory_space=pltpu.SMEM), vmem, vmem, vmem],
        out_specs=(vmem, vmem),
        scratch_shapes=[pltpu.VMEM((512, WIN), jnp.bfloat16)],
        compiler_params=pltpu.CompilerParams(vmem_limit_bytes=24 * 1024 * 1024),
        name="prepare",
    )(source_blocks, raw_data, row_owner.reshape(1, 64), jnp.asarray(forward_table(), jnp.float32))


MESH = pl.DeviceIdType.MESH
ORDER = (2, 1, 3, 0)


def exchange_kernel(slots, first, held, panels, staged, chunk, turn_send, turn_recv, xy_send, xy_recv, z_send, z_recv, pair_send, pair_recv,
                    core_send, core_recv, pz_send, pz_recv, pxy_send, pxy_recv, local_sem):
    recv = lax.axis_index("recv")
    seg = lax.axis_index("seg")
    y, x, zh = recv // 16, (recv // 4) % 4, recv % 4
    zl, core = seg // 2, seg % 2
    plane = y * 4 + x

    def plane_peer(step):
        return ((y + step // 4) % 4) * 4 + (x + step % 4) % 4

    def xy_copy(turn, step):
        target = plane_peer(step)
        block = (zh + turn) % 4
        return pltpu.make_async_remote_copy(
            src_ref=slots.at[target, block],
            dst_ref=staged.at[block, plane],
            send_sem=xy_send.at[turn, step],
            recv_sem=xy_recv.at[turn, step],
            device_id=(target * 4 + zh, seg),
            device_id_type=MESH,
        )

    near = (None, 0, 1 - zl, 1)

    def z_copy(turn, low):
        block = (zh + turn) % 4
        return pltpu.make_async_remote_copy(
            src_ref=staged.at[block],
            dst_ref=held.at[seg, :, zh],
            send_sem=z_send.at[turn],
            recv_sem=z_recv.at[turn, zl],
            device_id=(plane * 4 + block, low * 2 + core),
            device_id_type=MESH,
        )

    def z_arrival(turn, low):
        return pltpu.make_async_remote_copy(
            src_ref=staged.at[0],
            dst_ref=held.at[low * 2 + core, :, (zh + 4 - turn) % 4],
            send_sem=z_send.at[turn],
            recv_sem=z_recv.at[turn, low],
            device_id=(recv, seg),
            device_id_type=MESH,
        )

    def pair_copy(turn, low):
        place = held.at[low * 2 + core, :, (zh + 4 - turn) % 4]
        return pltpu.make_async_remote_copy(
            src_ref=place,
            dst_ref=place,
            send_sem=pair_send.at[turn, low],
            recv_sem=pair_recv.at[turn, low],
            device_id=(recv, (1 - zl) * 2 + core),
            device_id_type=MESH,
        )

    def core_copy(turn, low):
        place = (zh + 4 - turn) % 4
        return pltpu.make_async_remote_copy(
            src_ref=held.at[low * 2 + core, :, place],
            dst_ref=held.at[low * 2 + core, :, place],
            send_sem=core_send.at[turn, low],
            recv_sem=core_recv.at[turn, low],
            device_id=(recv, zl * 2 + 1 - core),
            device_id_type=MESH,
        )

    def pz_copy(turn):
        return pltpu.make_async_remote_copy(
            src_ref=chunk,
            dst_ref=panels.at[plane, zh],
            send_sem=pz_send.at[turn],
            recv_sem=pz_recv.at[turn],
            device_id=(plane * 4 + (zh + turn) % 4, seg),
            device_id_type=MESH,
        )

    def pxy_copy(step):
        return pltpu.make_async_remote_copy(
            src_ref=panels.at[plane],
            dst_ref=panels.at[plane],
            send_sem=pxy_send.at[step],
            recv_sem=pxy_recv.at[step],
            device_id=(plane_peer(step) * 4 + zh, seg),
            device_id_type=MESH,
        )

    def turn_copy():
        return pltpu.make_async_remote_copy(
            src_ref=first,
            dst_ref=chunk,
            send_sem=turn_send,
            recv_sem=turn_recv,
            device_id=((seg * 4 + x) * 4 + zh, y),
            device_id_type=MESH,
        )

    barrier = pltpu.get_barrier_semaphore()

    @pl.when(y != seg)
    def _():
        pl.semaphore_signal(barrier, inc=1, device_id=((seg * 4 + x) * 4 + zh, y), device_id_type=MESH)

    @pl.loop(1, 16)
    def _(step):
        pl.semaphore_signal(barrier, inc=1, device_id=(plane_peer(step) * 4 + zh, seg), device_id_type=MESH)

    @pl.loop(1, 8)
    def _(step):
        z = (zh * 2 + zl + step) % 8
        pl.semaphore_signal(
            barrier, inc=1, device_id=(plane * 4 + z // 2, (z % 2) * 2 + core), device_id_type=MESH
        )

    pl.semaphore_signal(barrier, inc=1, device_id=(recv, zl * 2 + 1 - core), device_id_type=MESH)
    kept_chunk = pltpu.make_async_copy(first, chunk, local_sem.at[6])
    own_chunk = pltpu.make_async_copy(chunk, panels.at[plane, zh], local_sem.at[4])

    @pl.when(y == seg)
    def _():
        kept_chunk.start()

    own = []
    for turn in ORDER:
        block = (zh + turn) % 4
        own.append(pltpu.make_async_copy(slots.at[plane, block], staged.at[block, plane], local_sem.at[turn]))
        own[-1].start()
    @pl.when(y == seg)
    def _():
        pl.semaphore_wait(barrier, 23)

    @pl.when(y != seg)
    def _():
        pl.semaphore_wait(barrier, 24)
        turn_copy().start()

    for turn in ORDER[:1]:
        @pl.loop(1, 16)
        def _(step):
            xy_copy(turn, step).start()
    for turn in ORDER[1:]:
        @pl.loop(1, 16)
        def _(step):
            xy_copy(turn, step).start()

    @pl.when(y != seg)
    def _():
        turn_copy().wait()

    @pl.when(y == seg)
    def _():
        kept_chunk.wait()

    own_chunk.start()
    for turn in (1, 2, 3):
        pz_copy(turn).start()

    kept = None
    for number, turn in enumerate(ORDER):
        own[number].wait()

        @pl.loop(1, 16)
        def _(step):
            xy_copy(turn, step).wait_recv()

        if turn:
            z_copy(turn, near[turn]).start()
        else:
            z_copy(0, 1 - zl).start()
            kept = pltpu.make_async_copy(
                staged.at[zh], held.at[seg, :, zh], local_sem.at[5]
            )
            kept.start()
        if number == 0:
            own_chunk.wait()
            for other in (1, 2, 3):
                pz_copy(other).wait_recv()

            @pl.loop(1, 16)
            def _(step):
                pxy_copy(step).start()

    kept.wait()
    core_copy(0, zl).start()
    direct, far = 1 + 2 * zl, 3 - 2 * zl
    for turn, low in ((2, 1 - zl), (direct, 0), (direct, 1)):
        z_arrival(turn, low).wait_recv()
        pair_copy(turn, low).start()
        core_copy(turn, low).start()
    z_arrival(0, 1 - zl).wait_recv()
    core_copy(0, 1 - zl).start()
    for turn, low in ((2, zl), (far, 0), (far, 1)):
        pair_copy(turn, low).wait_recv()
        core_copy(turn, low).start()

    @pl.loop(1, 16)
    def _(step):
        pxy_copy(step).wait_recv()
        pxy_copy(step).wait_send()
        for turn in ORDER:
            xy_copy(turn, step).wait_send()

    for turn in (1, 2, 3):
        pz_copy(turn).wait_send()
        z_copy(turn, near[turn]).wait_send()
    z_copy(0, 1 - zl).wait_send()
    for turn, low in ((2, 1 - zl), (direct, 0), (direct, 1)):
        pair_copy(turn, low).wait_send()
    for turn in range(4):
        for low in (0, 1):
            core_copy(turn, low).wait()


def exchange(slots, chunk):
    dma = pltpu.SemaphoreType.DMA
    rows, width = slots.shape[-2:]
    return pl.pallas_call(
        exchange_kernel,
        out_shape=(
            jax.ShapeDtypeStruct((4, 16, 4, rows, width), jnp.bfloat16),
            jax.ShapeDtypeStruct((16, 4) + chunk.shape, jnp.bfloat16),
        ),
        in_specs=[pl.BlockSpec(memory_space=pltpu.VMEM)] * 2,
        out_specs=(pl.BlockSpec(memory_space=pltpu.VMEM),) * 2,
        scratch_shapes=[
            pltpu.VMEM((4, 16, rows, width), jnp.bfloat16),
            pltpu.VMEM(chunk.shape, jnp.bfloat16),
            dma, dma, dma((4, 16)), dma((4, 16)), dma((4,)), dma((4, 2)), dma((4, 2)), dma((4, 2)),
            dma((4, 2)), dma((4, 2)),
            dma((4,)), dma((4,)), dma((16,)), dma((16,)), dma((7,)),
        ],
        compiler_params=pltpu.CompilerParams(
            collective_id=0, has_side_effects=True, vmem_limit_bytes=32 * 1024 * 1024
        ),
        name="exchange",
    )(slots, chunk)


NT=(((1,),(1,)),((),())); TN=(((0,),(0,)),((),()))
def body(held, panels, inv, out, x, rf, lt, ss, *, per):
    f32=jnp.float32; bf=jnp.bfloat16
    @pl.when(pl.program_id(0)==0)
    def _():
        row=lax.broadcasted_iota(jnp.int32,(256,256),0); col=lax.broadcasted_iota(jnp.int32,(256,256),1)
        eye=(row==col).astype(f32).astype(bf)
        def turned(n,c):
            return lax.dot_general(eye, x[pl.ds(pl.multiple_of(n*256,256),256),c*256:(c+1)*256], NT, preferred_element_type=f32)
        perm=((row%32)//2*16+row%2*8+row//32==col).astype(f32).astype(bf)
        @pl.loop(0,16,unroll=2)
        def _(n):
            k=n//4; g=n%4
            y=jnp.dot(perm, held[k,pl.ds(g*16,16)].reshape(256,512), preferred_element_type=f32).astype(bf)
            for w in range(8):
                x[pl.ds(pl.multiple_of((k*8+w)*128+g*32,32),32),:]=y[w*32:(w+1)*32]
        @pl.loop(0,16,unroll=2)
        def _(n):
            for c in range(2):
                v=turned(n,c)
                for dw in range(2):
                    rf[pl.ds(c*32+n*2+dw,256,stride=72),:]=v[:,dw*128:(dw+1)*128]
        perm2=((row%16)//2*32+(row%32)//16*16+row%2*8+row//32==col).astype(f32).astype(bf)
        @pl.loop(0,8,unroll=2)
        def _(n):
            k=n//2; g=n%2
            y=jnp.dot(perm2, panels[pl.ds(n*8,8)].reshape(256,512), preferred_element_type=f32).astype(bf)
            for w in range(8):
                for b in range(2):
                    for h in range(2):
                        x[pl.ds(pl.multiple_of((k*8+w)*128+h*64+b*32+g*16,16),16),:]=y[w*32+b*16:w*32+b*16+16]
        lane=lax.broadcasted_iota(jnp.int32,(256,128),1)<64
        first=lax.broadcasted_iota(jnp.int32,(256,128),0)==0
        @pl.loop(0,16,unroll=2)
        def _(n):
            real, imag = turned(n,0), turned(n,1)
            for dw in range(2):
                re=real[:,dw*128:(dw+1)*128]; im=imag[:,dw*128:(dw+1)*128]
                lt[pl.ds(n*2+dw,256,stride=72),:]=jnp.where(lane,re,jnp.where(first,0.0,-im))
                lt[pl.ds(32+n*2+dw,256,stride=72),:]=jnp.where(lane,jnp.where(first,0.0,im),jnp.where(first,im,re))
        @pl.loop(0,256,unroll=8)
        def _(j):
            at=pl.ds(pl.multiple_of(j*72,8),64)
            s=lax.dot_general(lt[at,:].astype(bf), rf[at,:].astype(bf), TN, preferred_element_type=f32)
            ss[pl.ds(j,64,stride=520),:]=s[:64]
            ss[pl.ds(256+j,64,stride=520),:]=s[64:]
    base=pl.program_id(0)*per
    @pl.loop(0,per,unroll=4)
    def _(i):
        v=ss[pl.ds(pl.multiple_of((base+i)*520,8),512),:].astype(bf)
        out[i]=lax.dot_general(v, inv[...], TN, preferred_element_type=f32).astype(bf)

def compute(held, panels, inv, per=8):
    one=pl.Buffered(1)
    def whole(a): return pl.BlockSpec(a.shape, lambda i: (0,)*a.ndim, pipeline_mode=one)
    return pl.pallas_call(functools.partial(body,per=per), grid=(64//per,),
        out_shape=jax.ShapeDtypeStruct((64,128,512),jnp.bfloat16),
        in_specs=[whole(held),whole(panels),whole(inv)],
        out_specs=pl.BlockSpec((per,128,512),lambda i:(i,0,0)),
        scratch_shapes=[pltpu.VMEM((4096,512),jnp.bfloat16),pltpu.VMEM((256*72,128),jnp.float32),
            pltpu.VMEM((256*72,128),jnp.float32),pltpu.VMEM((64*520,128),jnp.float32)],
        compiler_params=pltpu.CompilerParams(vmem_limit_bytes=56*1024*1024), name="correlate")(held,panels,inv)


def local(raw_data, row_owner, source_blocks):
    slots, chunk = prepare(raw_data, row_owner, source_blocks)
    held, panels = exchange(slots.reshape(16, 4, 16, WIN), chunk)
    inverse = jnp.asarray(inverse_table(32), jnp.bfloat16)
    lagged = compute(
        held.reshape(4, 64, 16, WIN), panels.reshape(64, 32, WIN), inverse
    )
    return lagged.reshape(2, 32, 128, WIN)


def solution(mesh):
    placed = (P("seg", "recv", None), P("recv", None), P())
    return jax.shard_map(
        local, mesh=mesh, in_specs=placed, out_specs=P(None, "seg", "recv", None), check_vma=False
    )
```

```python
import functools
import math

import jax
import jax.numpy as jnp
import numpy as np
from jax import lax
from jax.experimental import pallas as pl
from jax.experimental.pallas import tpu as pltpu
from jax.sharding import PartitionSpec as P

WIN = 512
NB = 128
HALF = 256
STEP = 72
PITCH = 520
NT = (((1,), (1,)), ((), ()))
TN = (((0,), (0,)), ((), ()))


def forward_table():
    sample, freq = np.arange(WIN), np.arange(HALF)
    angles = (sample[:, None] * freq[None, :] % WIN) * (2.0 * math.pi / WIN)
    parity = np.where(sample % 2 == 0, 1.0, -1.0)
    sines = np.where(freq[None, :] == 0, parity[:, None], -np.sin(angles))
    return np.concatenate([np.cos(angles), sines], axis=1)


def inverse_table(window_total):
    lag, freq = np.arange(WIN) - HALF, np.arange(HALF)
    angles = (freq[:, None] * lag[None, :] % WIN) * (2.0 * math.pi / WIN)
    factor = 1.0 / (WIN * math.sqrt(window_total * WIN))
    parity = np.where(lag % 2 == 0, 1.0, -1.0)
    zero = freq[:, None] == 0
    cosine_rows = np.where(zero, factor, 2.0 * factor * np.cos(angles))
    sine_rows = np.where(zero, factor * parity[None, :], -2.0 * factor * np.sin(angles))
    return np.concatenate([cosine_rows, sine_rows], axis=0)


def prepare_kernel(blocks, raw, owner, table, slots, chunk, spectra):
    row = lax.broadcasted_iota(jnp.int32, (64, 512), 0)
    lane = lax.broadcasted_iota(jnp.int32, (64, 512), 1)
    diagonal = row[:, :64] == lane[:, :64]
    owner_column = jnp.sum(jnp.where(diagonal, owner[...], 0), axis=1, keepdims=True)
    owner_row = jnp.sum(jnp.where(row == lane % 64, owner_column, 0), axis=0, keepdims=True)
    same = (owner_column == owner_row) & (row < lane % 64)
    rank = jnp.sum(same.astype(jnp.int32), axis=0, keepdims=True)
    target = (owner_row * 2 + rank) * 8 + lax.broadcasted_iota(jnp.int32, (1, 512), 1) // 64
    for window in range(8):
        parts = []
        for run in range(4):
            start = (window % 4 * 4 + run) * NB
            values = raw[window // 4, :, start : start + NB]
            amplitude = jnp.mean(jnp.abs(values), axis=-1, keepdims=True) + 1e-06
            parts.append(values / amplitude)
        spectra[window * 64 : window * 64 + 64, :] = jnp.dot(
            jnp.concatenate(parts, axis=1),
            table[...],
            precision=lax.Precision.HIGHEST,
            preferred_element_type=jnp.float32,
        ).astype(jnp.bfloat16)

    @pl.loop(0, 4)
    def _(part):
        placed = lax.broadcasted_iota(jnp.int32, (256, 512), 0) + part * 256 == target
        slots[pl.ds(pl.multiple_of(part * 256, 256), 256), :] = jnp.dot(
            placed.astype(jnp.float32).astype(jnp.bfloat16),
            spectra[...],
            preferred_element_type=jnp.float32,
        ).astype(jnp.bfloat16)

    for b in range(2):
        chunk[b * 16 : b * 16 + 16, :] = slots[pl.ds(pl.multiple_of(blocks[b] * 16, 16), 16), :]


def prepare(raw_data, row_owner, source_blocks):
    vmem = pl.BlockSpec(memory_space=pltpu.VMEM)
    return pl.pallas_call(
        prepare_kernel,
        out_shape=(
            jax.ShapeDtypeStruct((1024, WIN), jnp.bfloat16),
            jax.ShapeDtypeStruct((32, WIN), jnp.bfloat16),
        ),
        in_specs=[pl.BlockSpec(memory_space=pltpu.SMEM), vmem, vmem, vmem],
        out_specs=(vmem, vmem),
        scratch_shapes=[pltpu.VMEM((512, WIN), jnp.bfloat16)],
        compiler_params=pltpu.CompilerParams(vmem_limit_bytes=24 * 1024 * 1024),
        name="prepare",
    )(source_blocks, raw_data, row_owner.reshape(1, 64), jnp.asarray(forward_table(), jnp.float32))


MESH = pl.DeviceIdType.MESH
ORDER = (2, 1, 3, 0)


def exchange_kernel(slots, first, sources, receivers, held, panels, placed, turned, staged, chunk, turn_send, turn_recv, xy_send, xy_recv, z_send, z_recv, pair_send, pair_recv,
                    core_send, core_recv, pz_send, pz_recv, pxy_send, pxy_recv, local_sem):
    recv = lax.axis_index("recv")
    seg = lax.axis_index("seg")
    y, x, zh = recv // 16, (recv // 4) % 4, recv % 4
    zl, core = seg // 2, seg % 2
    plane = y * 4 + x

    def plane_peer(step):
        return ((y + step // 4) % 4) * 4 + (x + step % 4) % 4

    def xy_copy(turn, step):
        target = plane_peer(step)
        block = (zh + turn) % 4
        return pltpu.make_async_remote_copy(
            src_ref=slots.at[target, block],
            dst_ref=staged.at[block, plane],
            send_sem=xy_send.at[turn, step],
            recv_sem=xy_recv.at[turn, step],
            device_id=(target * 4 + zh, seg),
            device_id_type=MESH,
        )

    near = (None, 0, 1 - zl, 1)

    def z_copy(turn, low):
        block = (zh + turn) % 4
        return pltpu.make_async_remote_copy(
            src_ref=staged.at[block],
            dst_ref=held.at[seg, :, zh],
            send_sem=z_send.at[turn],
            recv_sem=z_recv.at[turn, zl],
            device_id=(plane * 4 + block, low * 2 + core),
            device_id_type=MESH,
        )

    def z_arrival(turn, low):
        return pltpu.make_async_remote_copy(
            src_ref=staged.at[0],
            dst_ref=held.at[low * 2 + core, :, (zh + 4 - turn) % 4],
            send_sem=z_send.at[turn],
            recv_sem=z_recv.at[turn, low],
            device_id=(recv, seg),
            device_id_type=MESH,
        )

    def pair_copy(turn, low):
        place = held.at[low * 2 + core, :, (zh + 4 - turn) % 4]
        return pltpu.make_async_remote_copy(
            src_ref=place,
            dst_ref=place,
            send_sem=pair_send.at[turn, low],
            recv_sem=pair_recv.at[turn, low],
            device_id=(recv, (1 - zl) * 2 + core),
            device_id_type=MESH,
        )

    def core_copy(turn, low):
        place = (zh + 4 - turn) % 4
        return pltpu.make_async_remote_copy(
            src_ref=held.at[low * 2 + core, :, place],
            dst_ref=held.at[low * 2 + core, :, place],
            send_sem=core_send.at[turn, low],
            recv_sem=core_recv.at[turn, low],
            device_id=(recv, zl * 2 + 1 - core),
            device_id_type=MESH,
        )

    def core_arrival(turn, low):
        place = held.at[low * 2 + 1 - core, :, (zh + 4 - turn) % 4]
        return pltpu.make_async_remote_copy(
            src_ref=place,
            dst_ref=place,
            send_sem=core_send.at[turn, low],
            recv_sem=core_recv.at[turn, low],
            device_id=(recv, seg),
            device_id_type=MESH,
        )

    def pz_copy(turn):
        return pltpu.make_async_remote_copy(
            src_ref=chunk,
            dst_ref=panels.at[plane, zh],
            send_sem=pz_send.at[turn],
            recv_sem=pz_recv.at[turn],
            device_id=(plane * 4 + (zh + turn) % 4, seg),
            device_id_type=MESH,
        )

    def pxy_copy(step):
        return pltpu.make_async_remote_copy(
            src_ref=panels.at[plane],
            dst_ref=panels.at[plane],
            send_sem=pxy_send.at[step],
            recv_sem=pxy_recv.at[step],
            device_id=(plane_peer(step) * 4 + zh, seg),
            device_id_type=MESH,
        )

    def turn_copy():
        return pltpu.make_async_remote_copy(
            src_ref=first,
            dst_ref=chunk,
            send_sem=turn_send,
            recv_sem=turn_recv,
            device_id=((seg * 4 + x) * 4 + zh, y),
            device_id_type=MESH,
        )

    row = lax.broadcasted_iota(jnp.int32, (256, 256), 0)
    column = lax.broadcasted_iota(jnp.int32, (256, 256), 1)

    def zero_one(hits):
        return hits.astype(jnp.float32).astype(jnp.bfloat16)

    def place_block(window_group, block):
        order = zero_one(row % 32 // 2 * 16 + row % 2 * 8 + row // 32 == column)
        rows = jnp.dot(
            order,
            held[window_group, :, block].reshape(256, WIN),
            preferred_element_type=jnp.float32,
        ).astype(jnp.bfloat16)
        for w in range(8):
            start = (window_group * 8 + w) * 128 + block * 32
            placed[pl.ds(pl.multiple_of(start, 32), 32), :] = rows[w * 32 : w * 32 + 32]

    def turn_receivers():
        channel = row % 128
        order = zero_one(
            (column // 128 == row // 128)
            & (column % 128 == channel % 32 // 2 * 8 + channel // 32 * 2 + channel % 2)
        )

        @pl.loop(0, 16, unroll=2)
        def _(n):
            for c in range(2):
                block = placed[pl.ds(pl.multiple_of(n * 256, 256), 256), c * HALF : c * HALF + HALF]
                part = lax.dot_general(block, order, TN, preferred_element_type=jnp.float32)
                for w in range(2):
                    receivers[pl.ds(c * 32 + n * 2 + w, HALF, stride=STEP), :] = part[
                        :, w * 128 : w * 128 + 128
                    ]

    def turn_sources(window_group):
        order = zero_one(row % 16 // 2 * 32 + row % 32 // 16 * 16 + row % 2 * 8 + row // 32 == column)
        same = zero_one(row == column)
        low_lane = lax.broadcasted_iota(jnp.int32, (HALF, 128), 1) < 64
        zero_row = lax.broadcasted_iota(jnp.int32, (HALF, 128), 0) == 0
        for g in range(2):
            block = panels[pl.ds(window_group * 4 + g * 2, 2)].reshape(256, WIN)
            rows = jnp.dot(order, block, preferred_element_type=jnp.float32).astype(jnp.bfloat16)
            for w in range(8):
                for b in range(2):
                    for copy in range(2):
                        start = w * 128 + copy * 64 + b * 32 + g * 16
                        turned[start : start + 16, :] = rows[w * 32 + b * 16 : w * 32 + b * 16 + 16]
        for n in range(4):
            real, imag = (
                lax.dot_general(
                    same,
                    turned[n * 256 : n * 256 + 256, c * HALF : c * HALF + HALF],
                    NT,
                    preferred_element_type=jnp.float32,
                )
                for c in range(2)
            )
            for w in range(2):
                re, im = real[:, w * 128 : w * 128 + 128], imag[:, w * 128 : w * 128 + 128]
                window = window_group * 8 + n * 2 + w
                sources[pl.ds(window, HALF, stride=STEP), :] = jnp.where(
                    low_lane, re, jnp.where(zero_row, 0.0, -im)
                )
                sources[pl.ds(32 + window, HALF, stride=STEP), :] = jnp.where(
                    low_lane, jnp.where(zero_row, 0.0, im), jnp.where(zero_row, im, re)
                )

    barrier = pltpu.get_barrier_semaphore()

    @pl.when(y != seg)
    def _():
        pl.semaphore_signal(barrier, inc=1, device_id=((seg * 4 + x) * 4 + zh, y), device_id_type=MESH)

    @pl.loop(1, 16)
    def _(step):
        pl.semaphore_signal(barrier, inc=1, device_id=(plane_peer(step) * 4 + zh, seg), device_id_type=MESH)

    @pl.loop(1, 8)
    def _(step):
        z = (zh * 2 + zl + step) % 8
        pl.semaphore_signal(
            barrier, inc=1, device_id=(plane * 4 + z // 2, (z % 2) * 2 + core), device_id_type=MESH
        )

    pl.semaphore_signal(barrier, inc=1, device_id=(recv, zl * 2 + 1 - core), device_id_type=MESH)
    kept_chunk = pltpu.make_async_copy(first, chunk, local_sem.at[6])
    own_chunk = pltpu.make_async_copy(chunk, panels.at[plane, zh], local_sem.at[4])

    @pl.when(y == seg)
    def _():
        kept_chunk.start()

    own = []
    for turn in ORDER:
        block = (zh + turn) % 4
        own.append(pltpu.make_async_copy(slots.at[plane, block], staged.at[block, plane], local_sem.at[turn]))
        own[-1].start()
    @pl.when(y == seg)
    def _():
        pl.semaphore_wait(barrier, 23)

    @pl.when(y != seg)
    def _():
        pl.semaphore_wait(barrier, 24)
        turn_copy().start()

    for turn in ORDER[:1]:
        @pl.loop(1, 16)
        def _(step):
            xy_copy(turn, step).start()
    for turn in ORDER[1:]:
        @pl.loop(1, 16)
        def _(step):
            xy_copy(turn, step).start()

    @pl.when(y != seg)
    def _():
        turn_copy().wait()

    @pl.when(y == seg)
    def _():
        kept_chunk.wait()

    own_chunk.start()
    for turn in (1, 2, 3):
        pz_copy(turn).start()

    kept = None
    for number, turn in enumerate(ORDER):
        own[number].wait()

        @pl.loop(1, 16)
        def _(step):
            xy_copy(turn, step).wait_recv()

        if turn:
            z_copy(turn, near[turn]).start()
        else:
            z_copy(0, 1 - zl).start()
            kept = pltpu.make_async_copy(
                staged.at[zh], held.at[seg, :, zh], local_sem.at[5]
            )
            kept.start()
        if number == 0:
            own_chunk.wait()
            for other in (1, 2, 3):
                pz_copy(other).wait_recv()

            @pl.loop(1, 16)
            def _(step):
                pxy_copy(step).start()

    kept.wait()
    core_copy(0, zl).start()
    direct, far = 1 + 2 * zl, 3 - 2 * zl
    for turn, low in ((2, 1 - zl), (direct, 0), (direct, 1)):
        z_arrival(turn, low).wait_recv()
        pair_copy(turn, low).start()
        core_copy(turn, low).start()
    z_arrival(0, 1 - zl).wait_recv()
    core_copy(0, 1 - zl).start()

    @pl.loop(1, 16)
    def _(step):
        pxy_copy(step).wait_recv()

    @pl.loop(0, 4)
    def _(window_group):
        turn_sources(window_group)

    early = ((0, zl), (2, 1 - zl), (direct, 0), (direct, 1), (0, 1 - zl))
    late = ((2, zl), (far, 0), (far, 1))
    for turn, low in early:
        place_block(low * 2 + core, (zh + 4 - turn) % 4)
    for turn, low in late:
        pair_copy(turn, low).wait_recv()
        core_copy(turn, low).start()
    for turn, low in late:
        place_block(low * 2 + core, (zh + 4 - turn) % 4)
    for turn in range(4):
        for low in (0, 1):
            core_arrival(turn, low).wait_recv()
            place_block(low * 2 + 1 - core, (zh + 4 - turn) % 4)
    turn_receivers()

    @pl.loop(1, 16)
    def _(step):
        pxy_copy(step).wait_send()
        for turn in ORDER:
            xy_copy(turn, step).wait_send()

    for turn in (1, 2, 3):
        pz_copy(turn).wait_send()
        z_copy(turn, near[turn]).wait_send()
    z_copy(0, 1 - zl).wait_send()
    for turn, low in ((2, 1 - zl), (direct, 0), (direct, 1)):
        pair_copy(turn, low).wait_send()
    for turn in range(4):
        for low in (0, 1):
            core_copy(turn, low).wait_send()


def exchange(slots, chunk):
    dma = pltpu.SemaphoreType.DMA
    rows, width = slots.shape[-2:]
    return pl.pallas_call(
        exchange_kernel,
        out_shape=(
            jax.ShapeDtypeStruct((HALF * STEP, 128), jnp.float32),
            jax.ShapeDtypeStruct((HALF * STEP, 128), jnp.float32),
        ),
        in_specs=[pl.BlockSpec(memory_space=pltpu.VMEM)] * 2,
        out_specs=(pl.BlockSpec(memory_space=pltpu.VMEM),) * 2,
        scratch_shapes=[
            pltpu.VMEM((4, 16, 4, rows, width), jnp.bfloat16),
            pltpu.VMEM((16, 4) + chunk.shape, jnp.bfloat16),
            pltpu.VMEM((4096, width), jnp.bfloat16),
            pltpu.VMEM((1024, width), jnp.bfloat16),
            pltpu.VMEM((4, 16, rows, width), jnp.bfloat16),
            pltpu.VMEM(chunk.shape, jnp.bfloat16),
            dma, dma, dma((4, 16)), dma((4, 16)), dma((4,)), dma((4, 2)), dma((4, 2)), dma((4, 2)),
            dma((4, 2)), dma((4, 2)),
            dma((4,)), dma((4,)), dma((16,)), dma((16,)), dma((7,)),
        ],
        compiler_params=pltpu.CompilerParams(
            collective_id=0, has_side_effects=True, vmem_limit_bytes=22 * 1024 * 1024
        ),
        name="exchange",
    )(slots, chunk)


def correlate_kernel(sources, receivers, inverse, out, stack, lagged, sent):
    @pl.loop(0, HALF, unroll=8)
    def _(j):
        at = pl.ds(pl.multiple_of(j * STEP, 8), 64)
        terms = lax.dot_general(
            sources[at, :].astype(jnp.bfloat16),
            receivers[at, :].astype(jnp.bfloat16),
            TN,
            preferred_element_type=jnp.float32,
        )
        stack[pl.ds(j, 64, stride=PITCH), :] = terms[:64]
        stack[pl.ds(HALF + j, 64, stride=PITCH), :] = terms[64:]

    def out_copy(group, slot):
        return pltpu.make_async_copy(lagged.at[slot], out.at[pl.ds(group * 8, 8)], sent.at[slot])

    @pl.loop(0, 4)
    def _(pair):
        for slot in range(2):
            group = pair * 2 + slot

            @pl.when(pair > 0)
            def _():
                out_copy(group - 2, slot).wait()

            @pl.loop(0, 8, unroll=4)
            def _(i):
                start = (group * 8 + i) * PITCH
                lagged[slot, i] = lax.dot_general(
                    stack[pl.ds(pl.multiple_of(start, 8), WIN), :].astype(jnp.bfloat16),
                    inverse[...],
                    TN,
                    preferred_element_type=jnp.float32,
                ).astype(jnp.bfloat16)

            out_copy(group, slot).start()

    for slot in range(2):
        out_copy(6 + slot, slot).wait()


def correlate(sources, receivers, inverse):
    return pl.pallas_call(
        correlate_kernel,
        out_shape=jax.ShapeDtypeStruct((64, 128, WIN), jnp.bfloat16),
        in_specs=[pl.BlockSpec(memory_space=pltpu.VMEM)] * 3,
        out_specs=pl.BlockSpec(memory_space=pl.ANY),
        scratch_shapes=[
            pltpu.VMEM((64 * PITCH, 128), jnp.float32),
            pltpu.VMEM((2, 8, 128, WIN), jnp.bfloat16),
            pltpu.SemaphoreType.DMA((2,)),
        ],
        compiler_params=pltpu.CompilerParams(vmem_limit_bytes=24 * 1024 * 1024),
        name="correlate",
    )(sources, receivers, inverse)


def local(raw_data, row_owner, source_blocks):
    slots, chunk = prepare(raw_data, row_owner, source_blocks)
    sources, receivers = exchange(slots.reshape(16, 4, 16, WIN), chunk)
    inverse = jnp.asarray(inverse_table(32), jnp.bfloat16)
    lagged = correlate(sources, receivers, inverse)
    return lagged.reshape(2, 32, 128, WIN)


def solution(mesh):
    placed = (P("seg", "recv", None), P("recv", None), P())
    return jax.shard_map(
        local, mesh=mesh, in_specs=placed, out_specs=P(None, "seg", "recv", None), check_vma=False
    )
```

```python
import functools
import math

import jax
import jax.numpy as jnp
import ml_dtypes
import numpy as np
from jax import lax
from jax.experimental import pallas as pl
from jax.experimental.pallas import tpu as pltpu
from jax.sharding import PartitionSpec as P

WIN = 512
NB = 128
HALF = 256
STEP = 72
PITCH = 520
NT = (((1,), (1,)), ((), ()))
TN = (((0,), (0,)), ((), ()))


def forward_table():
    sample, freq = np.arange(WIN), np.arange(HALF)
    angles = (sample[:, None] * freq[None, :] % WIN) * (2.0 * math.pi / WIN)
    parity = np.where(sample % 2 == 0, 1.0, -1.0)
    sines = np.where(freq[None, :] == 0, parity[:, None], -np.sin(angles))
    return np.concatenate([np.cos(angles), sines], axis=1)


def inverse_table(window_total):
    lag, freq = np.arange(WIN) - HALF, np.arange(HALF)
    angles = (freq[:, None] * lag[None, :] % WIN) * (2.0 * math.pi / WIN)
    factor = 1.0 / (WIN * math.sqrt(window_total * WIN))
    parity = np.where(lag % 2 == 0, 1.0, -1.0)
    zero = freq[:, None] == 0
    cosine_rows = np.where(zero, factor, 2.0 * factor * np.cos(angles))
    sine_rows = np.where(zero, factor * parity[None, :], -2.0 * factor * np.sin(angles))
    return np.concatenate([cosine_rows, sine_rows], axis=0)


def forward_halves():
    table = forward_table().astype(np.float32)
    high = table.astype(ml_dtypes.bfloat16)
    low = (table - high.astype(np.float32)).astype(ml_dtypes.bfloat16)
    return jnp.asarray(np.stack([high, low]))


ORDER = (2, 1, 3, 0)
GROUPS = ((0, 1), (1, 1), (2, 2))


def split(values):
    high = values.astype(jnp.bfloat16)
    return high, (values - high.astype(jnp.float32)).astype(jnp.bfloat16)


def product(left, right):
    return jnp.dot(left, right, preferred_element_type=jnp.float32)


def place_of(turn):
    place = 0
    for number, listed in enumerate(ORDER):
        place = place + number * (turn == listed).astype(jnp.int32)
    return place


def prepare_kernel(blocks_hbm, raw_hbm, owner_hbm, table_hbm, slots, chunk, blocks, raw, owner, table, spectra, sems):
    copies = [
        pltpu.make_async_copy(owner_hbm, owner, sems.at[0]),
        pltpu.make_async_copy(blocks_hbm, blocks, sems.at[1]),
        pltpu.make_async_copy(table_hbm.at[0], table.at[0], sems.at[2]),
        pltpu.make_async_copy(table_hbm.at[1], table.at[1], sems.at[3]),
    ]
    for piece in range(4):
        rows = pl.ds(piece % 2 * 32, 32)
        copies.append(
            pltpu.make_async_copy(
                raw_hbm.at[piece // 2, rows], raw.at[piece // 2, rows], sems.at[4 + piece]
            )
        )
    for copy in copies:
        copy.start()
    zh = lax.axis_index("recv") % 4
    row = lax.broadcasted_iota(jnp.int32, (64, 512), 0)
    lane = lax.broadcasted_iota(jnp.int32, (64, 512), 1)
    diagonal = row[:, :64] == lane[:, :64]
    copies[0].wait()
    owner_column = jnp.sum(jnp.where(diagonal, owner[...], 0), axis=1, keepdims=True)
    owner_row = jnp.sum(jnp.where(row == lane % 64, owner_column, 0), axis=0, keepdims=True)
    same = (owner_column == owner_row) & (row < lane % 64)
    rank = jnp.sum(same.astype(jnp.int32), axis=0, keepdims=True)
    place = owner_row // 4 * 4 + place_of((owner_row % 4 + 4 - zh) % 4)
    target = (place * 2 + rank) * 8 + lax.broadcasted_iota(jnp.int32, (1, 512), 1) // 64
    for copy in copies[1:]:
        copy.wait()
    for window in range(8):
        parts = []
        for run in range(4):
            start = (window % 4 * 4 + run) * NB
            values = raw[window // 4, :, start : start + NB]
            amplitude = jnp.mean(jnp.abs(values), axis=-1, keepdims=True) + 1e-06
            parts.append(values / amplitude)
        high, low = split(jnp.concatenate(parts, axis=1))
        spectra[window * 64 : window * 64 + 64, :] = (
            product(high, table[0]) + (product(low, table[0]) + product(high, table[1]))
        ).astype(jnp.bfloat16)

    @pl.loop(0, 4, unroll=2)
    def _(part):
        placed = lax.broadcasted_iota(jnp.int32, (256, 512), 0) + part * 256 == target
        slots[pl.ds(pl.multiple_of(part * 256, 256), 256), :] = product(
            placed.astype(jnp.float32).astype(jnp.bfloat16), spectra[...]
        ).astype(jnp.bfloat16)

    for b in range(2):
        block = blocks[b]
        start = (block // 4 * 4 + place_of((block % 4 + 4 - zh) % 4)) * 16
        chunk[b * 16 : b * 16 + 16, :] = slots[pl.ds(pl.multiple_of(start, 16), 16), :]


def prepare(raw_data, row_owner, source_blocks):
    hbm = pl.BlockSpec(memory_space=pltpu.HBM)
    vmem = pl.BlockSpec(memory_space=pltpu.VMEM)
    return pl.pallas_call(
        prepare_kernel,
        out_shape=(
            jax.ShapeDtypeStruct((1024, WIN), jnp.bfloat16),
            jax.ShapeDtypeStruct((32, WIN), jnp.bfloat16),
        ),
        in_specs=[hbm] * 4,
        out_specs=(vmem, vmem),
        scratch_shapes=[
            pltpu.SMEM((2,), jnp.int32),
            pltpu.VMEM(raw_data.shape, jnp.float32),
            pltpu.VMEM((1, 64), jnp.int32),
            pltpu.VMEM((2, WIN, WIN), jnp.bfloat16),
            pltpu.VMEM((512, WIN), jnp.bfloat16),
            pltpu.SemaphoreType.DMA((8,)),
        ],
        compiler_params=pltpu.CompilerParams(vmem_limit_bytes=60 * 1024 * 1024),
        name="prepare",
    )(source_blocks, raw_data, row_owner.reshape(1, 64), forward_halves())


MESH = pl.DeviceIdType.MESH


def exchange_kernel(slots, first, sources, receivers, held, panels, placed, turned, staged, chunk, turn_send, turn_recv, xy_send, xy_recv, z_send, z_recv, pair_send, pair_recv,
                    core_send, core_recv, pz_send, pz_recv, pxy_send, pxy_recv, local_sem):
    recv = lax.axis_index("recv")
    seg = lax.axis_index("seg")
    y, x, zh = recv // 16, (recv // 4) % 4, recv % 4
    zl, core = seg // 2, seg % 2
    plane = y * 4 + x

    def plane_peer(step):
        return ((y + step // 4) % 4) * 4 + (x + step % 4) % 4

    def xy_copy(group, step):
        target = plane_peer(step)
        start, count = GROUPS[group]
        places = pl.ds(start, count)
        return pltpu.make_async_remote_copy(
            src_ref=slots.at[target, places],
            dst_ref=staged.at[places, plane],
            send_sem=xy_send.at[group, step],
            recv_sem=xy_recv.at[group, step],
            device_id=(target * 4 + zh, seg),
            device_id_type=MESH,
        )

    near = (None, 0, 1 - zl, 1)

    def half_of(half):
        return pl.ds(half * 8, 8)

    def held_from(turn, low, owner_core, half):
        return held.at[low * 2 + owner_core, half_of(half), (zh + 4 - turn) % 4]

    def z_copy(turn, low, half):
        return pltpu.make_async_remote_copy(
            src_ref=staged.at[ORDER.index(turn), half_of(half)],
            dst_ref=held.at[seg, half_of(half), zh],
            send_sem=z_send.at[turn, half],
            recv_sem=z_recv.at[turn, zl, half],
            device_id=(plane * 4 + (zh + turn) % 4, low * 2 + core),
            device_id_type=MESH,
        )

    def z_arrival(turn, low, half):
        return pltpu.make_async_remote_copy(
            src_ref=staged.at[0, half_of(half)],
            dst_ref=held_from(turn, low, core, half),
            send_sem=z_send.at[turn, half],
            recv_sem=z_recv.at[turn, low, half],
            device_id=(recv, seg),
            device_id_type=MESH,
        )

    def pair_copy(turn, low, half):
        place = held_from(turn, low, core, half)
        return pltpu.make_async_remote_copy(
            src_ref=place,
            dst_ref=place,
            send_sem=pair_send.at[turn, low, half],
            recv_sem=pair_recv.at[turn, low, half],
            device_id=(recv, (1 - zl) * 2 + core),
            device_id_type=MESH,
        )

    def core_copy(turn, low, half):
        place = held_from(turn, low, core, half)
        return pltpu.make_async_remote_copy(
            src_ref=place,
            dst_ref=place,
            send_sem=core_send.at[turn, low, half],
            recv_sem=core_recv.at[turn, low, half],
            device_id=(recv, zl * 2 + 1 - core),
            device_id_type=MESH,
        )

    def core_arrival(turn, low, half):
        place = held_from(turn, low, 1 - core, half)
        return pltpu.make_async_remote_copy(
            src_ref=place,
            dst_ref=place,
            send_sem=core_send.at[turn, low, half],
            recv_sem=core_recv.at[turn, low, half],
            device_id=(recv, seg),
            device_id_type=MESH,
        )

    def pz_copy(turn):
        return pltpu.make_async_remote_copy(
            src_ref=chunk,
            dst_ref=panels.at[plane, zh],
            send_sem=pz_send.at[turn],
            recv_sem=pz_recv.at[turn],
            device_id=(plane * 4 + (zh + turn) % 4, seg),
            device_id_type=MESH,
        )

    def pxy_copy(step):
        return pltpu.make_async_remote_copy(
            src_ref=panels.at[plane],
            dst_ref=panels.at[plane],
            send_sem=pxy_send.at[step],
            recv_sem=pxy_recv.at[step],
            device_id=(plane_peer(step) * 4 + zh, seg),
            device_id_type=MESH,
        )

    def turn_copy():
        return pltpu.make_async_remote_copy(
            src_ref=first,
            dst_ref=chunk,
            send_sem=turn_send,
            recv_sem=turn_recv,
            device_id=((seg * 4 + x) * 4 + zh, y),
            device_id_type=MESH,
        )

    row = lax.broadcasted_iota(jnp.int32, (256, 256), 0)
    column = lax.broadcasted_iota(jnp.int32, (256, 256), 1)

    def zero_one(hits):
        return hits.astype(jnp.float32).astype(jnp.bfloat16)

    def place_block(window_group, block):
        order = zero_one(row % 32 // 2 * 16 + row % 2 * 8 + row // 32 == column)
        rows = jnp.dot(
            order,
            held[window_group, :, block].reshape(256, WIN),
            preferred_element_type=jnp.float32,
        ).astype(jnp.bfloat16)
        for w in range(8):
            start = (window_group * 8 + w) * 128 + block * 32
            placed[pl.ds(pl.multiple_of(start, 32), 32), :] = rows[w * 32 : w * 32 + 32]

    def turn_receivers():
        channel = row % 128
        order = zero_one(
            (column // 128 == row // 128)
            & (column % 128 == channel % 32 // 2 * 8 + channel // 32 * 2 + channel % 2)
        )

        @pl.loop(0, 16, unroll=2)
        def _(n):
            for c in range(2):
                block = placed[pl.ds(pl.multiple_of(n * 256, 256), 256), c * HALF : c * HALF + HALF]
                part = lax.dot_general(block, order, TN, preferred_element_type=jnp.float32)
                for w in range(2):
                    receivers[pl.ds(c * 32 + n * 2 + w, HALF, stride=STEP), :] = part[
                        :, w * 128 : w * 128 + 128
                    ]

    def turn_sources(window_group):
        order = zero_one(row % 16 // 2 * 32 + row % 32 // 16 * 16 + row % 2 * 8 + row // 32 == column)
        same = zero_one(row == column)
        low_lane = lax.broadcasted_iota(jnp.int32, (HALF, 128), 1) < 64
        zero_row = lax.broadcasted_iota(jnp.int32, (HALF, 128), 0) == 0
        for g in range(2):
            block = panels[pl.ds(window_group * 4 + g * 2, 2)].reshape(256, WIN)
            rows = jnp.dot(order, block, preferred_element_type=jnp.float32).astype(jnp.bfloat16)
            for w in range(8):
                for b in range(2):
                    for copy in range(2):
                        start = w * 128 + copy * 64 + b * 32 + g * 16
                        turned[start : start + 16, :] = rows[w * 32 + b * 16 : w * 32 + b * 16 + 16]
        for n in range(4):
            real, imag = (
                lax.dot_general(
                    same,
                    turned[n * 256 : n * 256 + 256, c * HALF : c * HALF + HALF],
                    NT,
                    preferred_element_type=jnp.float32,
                )
                for c in range(2)
            )
            for w in range(2):
                re, im = real[:, w * 128 : w * 128 + 128], imag[:, w * 128 : w * 128 + 128]
                window = window_group * 8 + n * 2 + w
                sources[pl.ds(window, HALF, stride=STEP), :] = jnp.where(
                    low_lane, re, jnp.where(zero_row, 0.0, -im)
                )
                sources[pl.ds(32 + window, HALF, stride=STEP), :] = jnp.where(
                    low_lane, jnp.where(zero_row, 0.0, im), jnp.where(zero_row, im, re)
                )

    barrier = pltpu.get_barrier_semaphore()

    @pl.when(y != seg)
    def _():
        pl.semaphore_signal(barrier, inc=1, device_id=((seg * 4 + x) * 4 + zh, y), device_id_type=MESH)

    @pl.loop(1, 16)
    def _(step):
        pl.semaphore_signal(barrier, inc=1, device_id=(plane_peer(step) * 4 + zh, seg), device_id_type=MESH)

    @pl.loop(1, 8)
    def _(step):
        z = (zh * 2 + zl + step) % 8
        pl.semaphore_signal(
            barrier, inc=1, device_id=(plane * 4 + z // 2, (z % 2) * 2 + core), device_id_type=MESH
        )

    pl.semaphore_signal(barrier, inc=1, device_id=(recv, zl * 2 + 1 - core), device_id_type=MESH)
    kept_chunk = pltpu.make_async_copy(first, chunk, local_sem.at[6])
    own_chunk = pltpu.make_async_copy(chunk, panels.at[plane, zh], local_sem.at[4])

    @pl.when(y == seg)
    def _():
        kept_chunk.start()

    own = pltpu.make_async_copy(slots.at[plane], staged.at[:, plane], local_sem.at[0])
    own.start()

    @pl.when(y == seg)
    def _():
        pl.semaphore_wait(barrier, 23)

    @pl.when(y != seg)
    def _():
        pl.semaphore_wait(barrier, 24)
        turn_copy().start()

    for group in range(len(GROUPS)):

        @pl.loop(1, 16)
        def _(step):
            xy_copy(group, step).start()

    @pl.when(y != seg)
    def _():
        turn_copy().wait()

    @pl.when(y == seg)
    def _():
        kept_chunk.wait()

    own_chunk.start()
    for turn in (1, 2, 3):
        pz_copy(turn).start()

    kept = pltpu.make_async_copy(staged.at[ORDER.index(0)], held.at[seg, :, zh], local_sem.at[5])
    own.wait()
    for group, (start, count) in enumerate(GROUPS):

        @pl.loop(1, 16)
        def _(step):
            xy_copy(group, step).wait_recv()

        for turn in ORDER[start : start + count]:
            for half in range(2):
                z_copy(turn, near[turn] if turn else 1 - zl, half).start()
            if not turn:
                kept.start()
        if group == 0:
            own_chunk.wait()
            for other in (1, 2, 3):
                pz_copy(other).wait_recv()

            @pl.loop(1, 16)
            def _(step):
                pxy_copy(step).start()

    kept.wait()
    for half in range(2):
        core_copy(0, zl, half).start()
    direct, far = 1 + 2 * zl, 3 - 2 * zl
    for turn, low in ((2, 1 - zl), (direct, 0), (direct, 1)):
        for half in range(2):
            z_arrival(turn, low, half).wait_recv()
            pair_copy(turn, low, half).start()
            core_copy(turn, low, half).start()
    for half in range(2):
        z_arrival(0, 1 - zl, half).wait_recv()
        core_copy(0, 1 - zl, half).start()

    early = ((0, zl), (2, 1 - zl), (direct, 0), (direct, 1), (0, 1 - zl))
    late = ((2, zl), (far, 0), (far, 1))
    for turn, low in early:
        place_block(low * 2 + core, (zh + 4 - turn) % 4)
    for turn, low in early:
        for half in range(2):
            core_arrival(turn, low, half).wait_recv()
        place_block(low * 2 + 1 - core, (zh + 4 - turn) % 4)

    @pl.loop(1, 16)
    def _(step):
        pxy_copy(step).wait_recv()

    @pl.loop(0, 4)
    def _(window_group):
        turn_sources(window_group)

    for turn, low in late:
        for half in range(2):
            pair_copy(turn, low, half).wait_recv()
            core_copy(turn, low, half).start()
        place_block(low * 2 + core, (zh + 4 - turn) % 4)
    for turn, low in late:
        for half in range(2):
            core_arrival(turn, low, half).wait_recv()
        place_block(low * 2 + 1 - core, (zh + 4 - turn) % 4)
    turn_receivers()

    @pl.loop(1, 16)
    def _(step):
        pxy_copy(step).wait_send()
        for group in range(len(GROUPS)):
            xy_copy(group, step).wait_send()

    for turn in (1, 2, 3):
        pz_copy(turn).wait_send()
    for half in range(2):
        for turn in range(4):
            z_copy(turn, near[turn] if turn else 1 - zl, half).wait_send()
            for low in (0, 1):
                core_copy(turn, low, half).wait_send()
        for turn, low in ((2, 1 - zl), (direct, 0), (direct, 1)):
            pair_copy(turn, low, half).wait_send()


def exchange(slots, chunk):
    dma = pltpu.SemaphoreType.DMA
    rows, width = slots.shape[-2:]
    return pl.pallas_call(
        exchange_kernel,
        out_shape=(
            jax.ShapeDtypeStruct((HALF * STEP, 128), jnp.float32),
            jax.ShapeDtypeStruct((HALF * STEP, 128), jnp.float32),
        ),
        in_specs=[pl.BlockSpec(memory_space=pltpu.VMEM)] * 2,
        out_specs=(pl.BlockSpec(memory_space=pltpu.VMEM),) * 2,
        scratch_shapes=[
            pltpu.VMEM((4, 16, 4, rows, width), jnp.bfloat16),
            pltpu.VMEM((16, 4) + chunk.shape, jnp.bfloat16),
            pltpu.VMEM((4096, width), jnp.bfloat16),
            pltpu.VMEM((1024, width), jnp.bfloat16),
            pltpu.VMEM((4, 16, rows, width), jnp.bfloat16),
            pltpu.VMEM(chunk.shape, jnp.bfloat16),
            dma, dma, dma((4, 16)), dma((4, 16)), dma((4, 2)), dma((4, 2, 2)),
            dma((4, 2, 2)), dma((4, 2, 2)), dma((4, 2, 2)), dma((4, 2, 2)),
            dma((4,)), dma((4,)), dma((16,)), dma((16,)), dma((7,)),
        ],
        compiler_params=pltpu.CompilerParams(
            collective_id=0, has_side_effects=True, vmem_limit_bytes=22 * 1024 * 1024
        ),
        name="exchange",
    )(slots, chunk)


def correlate_kernel(sources, receivers, inverse_hbm, out, stack, lagged, inverse, sent):
    table_copy = pltpu.make_async_copy(inverse_hbm, inverse, sent.at[2])
    table_copy.start()

    @pl.loop(0, HALF, unroll=8)
    def _(j):
        at = pl.ds(pl.multiple_of(j * STEP, 8), 64)
        terms = lax.dot_general(
            sources[at, :].astype(jnp.bfloat16),
            receivers[at, :].astype(jnp.bfloat16),
            TN,
            preferred_element_type=jnp.float32,
        )
        stack[pl.ds(j, 64, stride=PITCH), :] = terms[:64]
        stack[pl.ds(HALF + j, 64, stride=PITCH), :] = terms[64:]

    def out_copy(group, slot):
        return pltpu.make_async_copy(lagged.at[slot], out.at[pl.ds(group * 8, 8)], sent.at[slot])

    table_copy.wait()

    @pl.loop(0, 4)
    def _(pair):
        for slot in range(2):
            group = pair * 2 + slot

            @pl.when(pair > 0)
            def _():
                out_copy(group - 2, slot).wait()

            @pl.loop(0, 8, unroll=4)
            def _(i):
                start = (group * 8 + i) * PITCH
                lagged[slot, i] = lax.dot_general(
                    stack[pl.ds(pl.multiple_of(start, 8), WIN), :].astype(jnp.bfloat16),
                    inverse[...],
                    TN,
                    preferred_element_type=jnp.float32,
                ).astype(jnp.bfloat16)

            out_copy(group, slot).start()

    for slot in range(2):
        out_copy(6 + slot, slot).wait()


def correlate(sources, receivers, inverse):
    return pl.pallas_call(
        correlate_kernel,
        out_shape=jax.ShapeDtypeStruct((64, 128, WIN), jnp.bfloat16),
        in_specs=[pl.BlockSpec(memory_space=pltpu.VMEM)] * 2 + [pl.BlockSpec(memory_space=pltpu.HBM)],
        out_specs=pl.BlockSpec(memory_space=pl.ANY),
        scratch_shapes=[
            pltpu.VMEM((64 * PITCH, 128), jnp.float32),
            pltpu.VMEM((2, 8, 128, WIN), jnp.bfloat16),
            pltpu.VMEM((WIN, WIN), jnp.bfloat16),
            pltpu.SemaphoreType.DMA((3,)),
        ],
        compiler_params=pltpu.CompilerParams(vmem_limit_bytes=24 * 1024 * 1024),
        name="correlate",
    )(sources, receivers, inverse)


def local(raw_data, row_owner, source_blocks):
    slots, chunk = prepare(raw_data, row_owner, source_blocks)
    sources, receivers = exchange(slots.reshape(16, 4, 16, WIN), chunk)
    inverse = jnp.asarray(inverse_table(32), jnp.bfloat16)
    lagged = correlate(sources, receivers, inverse)
    return lagged.reshape(2, 32, 128, WIN)


def solution(mesh):
    placed = (P("seg", "recv", None), P("recv", None), P())
    return jax.shard_map(
        local, mesh=mesh, in_specs=placed, out_specs=P(None, "seg", "recv", None), check_vma=False
    )
```

```python
import functools
import math

import jax
import jax.numpy as jnp
import ml_dtypes
import numpy as np
from jax import lax
from jax.experimental import pallas as pl
from jax.experimental.pallas import tpu as pltpu
from jax.sharding import PartitionSpec as P

WIN = 512
NB = 128
HALF = 256
STEP = 72
PITCH = 520
NT = (((1,), (1,)), ((), ()))
TN = (((0,), (0,)), ((), ()))


def forward_table():
    sample, freq = np.arange(WIN), np.arange(HALF)
    angles = (sample[:, None] * freq[None, :] % WIN) * (2.0 * math.pi / WIN)
    parity = np.where(sample % 2 == 0, 1.0, -1.0)
    sines = np.where(freq[None, :] == 0, parity[:, None], -np.sin(angles))
    return np.concatenate([np.cos(angles), sines], axis=1)


def inverse_table(window_total):
    lag, freq = np.arange(WIN) - HALF, np.arange(HALF)
    angles = (freq[:, None] * lag[None, :] % WIN) * (2.0 * math.pi / WIN)
    factor = 1.0 / (WIN * math.sqrt(window_total * WIN))
    parity = np.where(lag % 2 == 0, 1.0, -1.0)
    zero = freq[:, None] == 0
    cosine_rows = np.where(zero, factor, 2.0 * factor * np.cos(angles))
    sine_rows = np.where(zero, factor * parity[None, :], -2.0 * factor * np.sin(angles))
    return np.concatenate([cosine_rows, sine_rows], axis=0)


def forward_halves():
    table = forward_table().astype(np.float32)
    high = table.astype(ml_dtypes.bfloat16)
    low = (table - high.astype(np.float32)).astype(ml_dtypes.bfloat16)
    return jnp.asarray(np.stack([high, low]))


ORDER = (2, 1, 3, 0)
GROUPS = ((0, 1), (1, 1), (2, 2))


def split(values):
    high = values.astype(jnp.bfloat16)
    return high, (values - high.astype(jnp.float32)).astype(jnp.bfloat16)


def product(left, right):
    return jnp.dot(left, right, preferred_element_type=jnp.float32)


def place_of(turn):
    place = 0
    for number, listed in enumerate(ORDER):
        place = place + number * (turn == listed).astype(jnp.int32)
    return place


def start_reads(blocks_hbm, raw_hbm, owner_hbm, table_hbm, blocks, raw, owner, table, sems):
    copies = [
        pltpu.make_async_copy(owner_hbm, owner, sems.at[0]),
        pltpu.make_async_copy(blocks_hbm, blocks, sems.at[1]),
        pltpu.make_async_copy(table_hbm.at[0], table.at[0], sems.at[2]),
        pltpu.make_async_copy(table_hbm.at[1], table.at[1], sems.at[3]),
    ]
    for piece in range(4):
        rows = pl.ds(piece % 2 * 32, 32)
        copies.append(
            pltpu.make_async_copy(
                raw_hbm.at[piece // 2, rows], raw.at[piece // 2, rows], sems.at[4 + piece]
            )
        )
    for copy in copies:
        copy.start()
    return copies


def prepare(copies, zh, blocks, raw, owner, table, slots, first, spectra):
    row = lax.broadcasted_iota(jnp.int32, (64, 512), 0)
    lane = lax.broadcasted_iota(jnp.int32, (64, 512), 1)
    diagonal = row[:, :64] == lane[:, :64]
    copies[0].wait()
    owner_column = jnp.sum(jnp.where(diagonal, owner[...], 0), axis=1, keepdims=True)
    owner_row = jnp.sum(jnp.where(row == lane % 64, owner_column, 0), axis=0, keepdims=True)
    same = (owner_column == owner_row) & (row < lane % 64)
    rank = jnp.sum(same.astype(jnp.int32), axis=0, keepdims=True)
    place = owner_row // 4 * 4 + place_of((owner_row % 4 + 4 - zh) % 4)
    target = (place * 2 + rank) * 8 + lax.broadcasted_iota(jnp.int32, (1, 512), 1) // 64
    for copy in copies[1:]:
        copy.wait()
    for window in range(8):
        parts = []
        for run in range(4):
            start = (window % 4 * 4 + run) * NB
            values = raw[window // 4, :, start : start + NB]
            amplitude = jnp.mean(jnp.abs(values), axis=-1, keepdims=True) + 1e-06
            parts.append(values / amplitude)
        high, low = split(jnp.concatenate(parts, axis=1))
        spectra[window * 64 : window * 64 + 64, :] = (
            product(high, table[0]) + (product(low, table[0]) + product(high, table[1]))
        ).astype(jnp.bfloat16)

    @pl.loop(0, 4, unroll=2)
    def _(part):
        placed = lax.broadcasted_iota(jnp.int32, (256, 512), 0) + part * 256 == target
        slots[pl.ds(part * 4, 4)] = product(
            placed.astype(jnp.float32).astype(jnp.bfloat16), spectra[...]
        ).astype(jnp.bfloat16).reshape(4, 4, 16, WIN)

    for b in range(2):
        block = blocks[b]
        first[b * 16 : b * 16 + 16, :] = slots[block // 4, place_of((block % 4 + 4 - zh) % 4)]


MESH = pl.DeviceIdType.MESH


def exchange_kernel(blocks_hbm, raw_hbm, owner_hbm, table_hbm, sources, receivers, blocks, raw, owner, table,
                    spectra, read_sem, slots, first, held, panels, placed, turned, staged, chunk, turn_send, turn_recv, xy_send, xy_recv, z_send, z_recv, pair_send, pair_recv,
                    core_send, core_recv, pz_send, pz_recv, pxy_send, pxy_recv, local_sem):
    reads = start_reads(blocks_hbm, raw_hbm, owner_hbm, table_hbm, blocks, raw, owner, table, read_sem)
    recv = lax.axis_index("recv")
    seg = lax.axis_index("seg")
    y, x, zh = recv // 16, (recv // 4) % 4, recv % 4
    zl, core = seg // 2, seg % 2
    plane = y * 4 + x

    def plane_peer(step):
        return ((y + step // 4) % 4) * 4 + (x + step % 4) % 4

    def xy_copy(group, step):
        target = plane_peer(step)
        start, count = GROUPS[group]
        places = pl.ds(start, count)
        return pltpu.make_async_remote_copy(
            src_ref=slots.at[target, places],
            dst_ref=staged.at[places, plane],
            send_sem=xy_send.at[group, step],
            recv_sem=xy_recv.at[group, step],
            device_id=(target * 4 + zh, seg),
            device_id_type=MESH,
        )

    near = (None, 0, 1 - zl, 1)

    def half_of(half):
        return pl.ds(half * 8, 8)

    def held_from(turn, low, owner_core, half):
        return held.at[low * 2 + owner_core, half_of(half), (zh + 4 - turn) % 4]

    def z_copy(turn, low, half):
        return pltpu.make_async_remote_copy(
            src_ref=staged.at[ORDER.index(turn), half_of(half)],
            dst_ref=held.at[seg, half_of(half), zh],
            send_sem=z_send.at[turn, half],
            recv_sem=z_recv.at[turn, zl, half],
            device_id=(plane * 4 + (zh + turn) % 4, low * 2 + core),
            device_id_type=MESH,
        )

    def z_arrival(turn, low, half):
        return pltpu.make_async_remote_copy(
            src_ref=staged.at[0, half_of(half)],
            dst_ref=held_from(turn, low, core, half),
            send_sem=z_send.at[turn, half],
            recv_sem=z_recv.at[turn, low, half],
            device_id=(recv, seg),
            device_id_type=MESH,
        )

    def pair_copy(turn, low, half):
        place = held_from(turn, low, core, half)
        return pltpu.make_async_remote_copy(
            src_ref=place,
            dst_ref=place,
            send_sem=pair_send.at[turn, low, half],
            recv_sem=pair_recv.at[turn, low, half],
            device_id=(recv, (1 - zl) * 2 + core),
            device_id_type=MESH,
        )

    def core_copy(turn, low, half):
        place = held_from(turn, low, core, half)
        return pltpu.make_async_remote_copy(
            src_ref=place,
            dst_ref=place,
            send_sem=core_send.at[turn, low, half],
            recv_sem=core_recv.at[turn, low, half],
            device_id=(recv, zl * 2 + 1 - core),
            device_id_type=MESH,
        )

    def core_arrival(turn, low, half):
        place = held_from(turn, low, 1 - core, half)
        return pltpu.make_async_remote_copy(
            src_ref=place,
            dst_ref=place,
            send_sem=core_send.at[turn, low, half],
            recv_sem=core_recv.at[turn, low, half],
            device_id=(recv, seg),
            device_id_type=MESH,
        )

    def pz_copy(turn):
        return pltpu.make_async_remote_copy(
            src_ref=chunk,
            dst_ref=panels.at[plane, zh],
            send_sem=pz_send.at[turn],
            recv_sem=pz_recv.at[turn],
            device_id=(plane * 4 + (zh + turn) % 4, seg),
            device_id_type=MESH,
        )

    def pxy_copy(step):
        return pltpu.make_async_remote_copy(
            src_ref=panels.at[plane],
            dst_ref=panels.at[plane],
            send_sem=pxy_send.at[step],
            recv_sem=pxy_recv.at[step],
            device_id=(plane_peer(step) * 4 + zh, seg),
            device_id_type=MESH,
        )

    def turn_copy():
        return pltpu.make_async_remote_copy(
            src_ref=first,
            dst_ref=chunk,
            send_sem=turn_send,
            recv_sem=turn_recv,
            device_id=((seg * 4 + x) * 4 + zh, y),
            device_id_type=MESH,
        )

    row = lax.broadcasted_iota(jnp.int32, (256, 256), 0)
    column = lax.broadcasted_iota(jnp.int32, (256, 256), 1)

    def zero_one(hits):
        return hits.astype(jnp.float32).astype(jnp.bfloat16)

    def place_block(window_group, block):
        order = zero_one(row % 32 // 2 * 16 + row % 2 * 8 + row // 32 == column)
        rows = jnp.dot(
            order,
            held[window_group, :, block].reshape(256, WIN),
            preferred_element_type=jnp.float32,
        ).astype(jnp.bfloat16)
        for w in range(8):
            start = (window_group * 8 + w) * 128 + block * 32
            placed[pl.ds(pl.multiple_of(start, 32), 32), :] = rows[w * 32 : w * 32 + 32]

    def turn_receivers():
        channel = row % 128
        order = zero_one(
            (column // 128 == row // 128)
            & (column % 128 == channel % 32 // 2 * 8 + channel // 32 * 2 + channel % 2)
        )

        @pl.loop(0, 16, unroll=4)
        def _(n):
            for c in range(2):
                block = placed[pl.ds(pl.multiple_of(n * 256, 256), 256), c * HALF : c * HALF + HALF]
                part = lax.dot_general(block, order, TN, preferred_element_type=jnp.float32)
                for w in range(2):
                    receivers[pl.ds(c * 32 + n * 2 + w, HALF, stride=STEP), :] = part[
                        :, w * 128 : w * 128 + 128
                    ]

    def turn_sources(window_group):
        order = zero_one(row % 16 // 2 * 32 + row % 32 // 16 * 16 + row % 2 * 8 + row // 32 == column)
        same = zero_one(row == column)
        low_lane = lax.broadcasted_iota(jnp.int32, (HALF, 128), 1) < 64
        zero_row = lax.broadcasted_iota(jnp.int32, (HALF, 128), 0) == 0
        for g in range(2):
            block = panels[pl.ds(window_group * 4 + g * 2, 2)].reshape(256, WIN)
            rows = jnp.dot(order, block, preferred_element_type=jnp.float32).astype(jnp.bfloat16)
            for w in range(8):
                for b in range(2):
                    for copy in range(2):
                        start = w * 128 + copy * 64 + b * 32 + g * 16
                        turned[start : start + 16, :] = rows[w * 32 + b * 16 : w * 32 + b * 16 + 16]
        for n in range(4):
            real, imag = (
                lax.dot_general(
                    same,
                    turned[n * 256 : n * 256 + 256, c * HALF : c * HALF + HALF],
                    NT,
                    preferred_element_type=jnp.float32,
                )
                for c in range(2)
            )
            for w in range(2):
                re, im = real[:, w * 128 : w * 128 + 128], imag[:, w * 128 : w * 128 + 128]
                window = window_group * 8 + n * 2 + w
                sources[pl.ds(window, HALF, stride=STEP), :] = jnp.where(
                    low_lane, re, jnp.where(zero_row, 0.0, -im)
                )
                sources[pl.ds(32 + window, HALF, stride=STEP), :] = jnp.where(
                    low_lane, jnp.where(zero_row, 0.0, im), jnp.where(zero_row, im, re)
                )

    barrier = pltpu.get_barrier_semaphore()

    @pl.when(y != seg)
    def _():
        pl.semaphore_signal(barrier, inc=1, device_id=((seg * 4 + x) * 4 + zh, y), device_id_type=MESH)

    @pl.loop(1, 16)
    def _(step):
        pl.semaphore_signal(barrier, inc=1, device_id=(plane_peer(step) * 4 + zh, seg), device_id_type=MESH)

    @pl.loop(1, 8)
    def _(step):
        z = (zh * 2 + zl + step) % 8
        pl.semaphore_signal(
            barrier, inc=1, device_id=(plane * 4 + z // 2, (z % 2) * 2 + core), device_id_type=MESH
        )

    pl.semaphore_signal(barrier, inc=1, device_id=(recv, zl * 2 + 1 - core), device_id_type=MESH)
    prepare(reads, zh, blocks, raw, owner, table, slots, first, spectra)
    kept_chunk = pltpu.make_async_copy(first, chunk, local_sem.at[6])
    own_chunk = pltpu.make_async_copy(chunk, panels.at[plane, zh], local_sem.at[4])

    @pl.when(y == seg)
    def _():
        kept_chunk.start()

    own = pltpu.make_async_copy(slots.at[plane], staged.at[:, plane], local_sem.at[0])
    own.start()

    @pl.when(y == seg)
    def _():
        pl.semaphore_wait(barrier, 23)

    @pl.when(y != seg)
    def _():
        pl.semaphore_wait(barrier, 24)
        turn_copy().start()

    for group in range(len(GROUPS)):

        @pl.loop(1, 16)
        def _(step):
            xy_copy(group, step).start()

    @pl.when(y != seg)
    def _():
        turn_copy().wait()

    @pl.when(y == seg)
    def _():
        kept_chunk.wait()

    own_chunk.start()
    for turn in (1, 2, 3):
        pz_copy(turn).start()

    kept = pltpu.make_async_copy(staged.at[ORDER.index(0)], held.at[seg, :, zh], local_sem.at[5])
    own.wait()
    for group, (start, count) in enumerate(GROUPS):

        @pl.loop(1, 16)
        def _(step):
            xy_copy(group, step).wait_recv()

        for turn in ORDER[start : start + count]:
            for half in range(2):
                z_copy(turn, near[turn] if turn else 1 - zl, half).start()
            if not turn:
                kept.start()
        if group == 0:
            own_chunk.wait()
            for other in (1, 2, 3):
                pz_copy(other).wait_recv()

            @pl.loop(1, 16)
            def _(step):
                pxy_copy(step).start()

    kept.wait()
    for half in range(2):
        core_copy(0, zl, half).start()
    direct, far = 1 + 2 * zl, 3 - 2 * zl
    for turn, low in ((2, 1 - zl), (direct, 0), (direct, 1)):
        for half in range(2):
            z_arrival(turn, low, half).wait_recv()
            pair_copy(turn, low, half).start()
            core_copy(turn, low, half).start()
    for half in range(2):
        z_arrival(0, 1 - zl, half).wait_recv()
        core_copy(0, 1 - zl, half).start()

    early = ((0, zl), (2, 1 - zl), (direct, 0), (direct, 1), (0, 1 - zl))
    late = ((2, zl), (far, 0), (far, 1))
    for turn, low in early:
        place_block(low * 2 + core, (zh + 4 - turn) % 4)
    for turn, low in early:
        for half in range(2):
            core_arrival(turn, low, half).wait_recv()
        place_block(low * 2 + 1 - core, (zh + 4 - turn) % 4)

    @pl.loop(1, 16)
    def _(step):
        pxy_copy(step).wait_recv()

    @pl.loop(0, 4)
    def _(window_group):
        turn_sources(window_group)

    for turn, low in late:
        for half in range(2):
            pair_copy(turn, low, half).wait_recv()
            core_copy(turn, low, half).start()
        place_block(low * 2 + core, (zh + 4 - turn) % 4)
    for turn, low in late:
        for half in range(2):
            core_arrival(turn, low, half).wait_recv()
        place_block(low * 2 + 1 - core, (zh + 4 - turn) % 4)
    turn_receivers()

    @pl.loop(1, 16)
    def _(step):
        pxy_copy(step).wait_send()
        for group in range(len(GROUPS)):
            xy_copy(group, step).wait_send()

    for turn in (1, 2, 3):
        pz_copy(turn).wait_send()
    for half in range(2):
        for turn in range(4):
            z_copy(turn, near[turn] if turn else 1 - zl, half).wait_send()
            for low in (0, 1):
                core_copy(turn, low, half).wait_send()
        for turn, low in ((2, 1 - zl), (direct, 0), (direct, 1)):
            pair_copy(turn, low, half).wait_send()


def exchange(raw_data, row_owner, source_blocks):
    dma = pltpu.SemaphoreType.DMA
    bf16 = jnp.bfloat16
    return pl.pallas_call(
        exchange_kernel,
        out_shape=(
            jax.ShapeDtypeStruct((HALF * STEP, 128), jnp.float32),
            jax.ShapeDtypeStruct((HALF * STEP, 128), jnp.float32),
        ),
        in_specs=[pl.BlockSpec(memory_space=pltpu.HBM)] * 4,
        out_specs=(pl.BlockSpec(memory_space=pltpu.VMEM),) * 2,
        scratch_shapes=[
            pltpu.SMEM((2,), jnp.int32),
            pltpu.VMEM(raw_data.shape, jnp.float32),
            pltpu.VMEM((1, 64), jnp.int32),
            pltpu.VMEM((2, WIN, WIN), bf16),
            pltpu.VMEM((512, WIN), bf16),
            dma((8,)),
            pltpu.VMEM((16, 4, 16, WIN), bf16),
            pltpu.VMEM((32, WIN), bf16),
            pltpu.VMEM((4, 16, 4, 16, WIN), bf16),
            pltpu.VMEM((16, 4, 32, WIN), bf16),
            pltpu.VMEM((4096, WIN), bf16),
            pltpu.VMEM((1024, WIN), bf16),
            pltpu.VMEM((4, 16, 16, WIN), bf16),
            pltpu.VMEM((32, WIN), bf16),
            dma, dma, dma((4, 16)), dma((4, 16)), dma((4, 2)), dma((4, 2, 2)),
            dma((4, 2, 2)), dma((4, 2, 2)), dma((4, 2, 2)), dma((4, 2, 2)),
            dma((4,)), dma((4,)), dma((16,)), dma((16,)), dma((7,)),
        ],
        compiler_params=pltpu.CompilerParams(
            collective_id=0, has_side_effects=True, vmem_limit_bytes=24576 * 1024
        ),
        name="exchange",
    )(source_blocks, raw_data, row_owner.reshape(1, 64), forward_halves())


def correlate_kernel(sources, receivers, inverse_hbm, out, stack, lagged, inverse, sent):
    table_copy = pltpu.make_async_copy(inverse_hbm, inverse, sent.at[2])
    table_copy.start()

    @pl.loop(0, HALF, unroll=32)
    def _(j):
        at = pl.ds(pl.multiple_of(j * STEP, 8), 64)
        terms = lax.dot_general(
            sources[at, :].astype(jnp.bfloat16),
            receivers[at, :].astype(jnp.bfloat16),
            TN,
            preferred_element_type=jnp.float32,
        )
        stack[pl.ds(j, 64, stride=PITCH), :] = terms[:64]
        stack[pl.ds(HALF + j, 64, stride=PITCH), :] = terms[64:]

    def out_copy(group, slot):
        return pltpu.make_async_copy(lagged.at[slot], out.at[pl.ds(group * 8, 8)], sent.at[slot])

    table_copy.wait()

    @pl.loop(0, 4)
    def _(pair):
        for slot in range(2):
            group = pair * 2 + slot

            @pl.when(pair > 0)
            def _():
                out_copy(group - 2, slot).wait()

            @pl.loop(0, 8, unroll=8)
            def _(i):
                start = (group * 8 + i) * PITCH
                lagged[slot, i] = lax.dot_general(
                    stack[pl.ds(pl.multiple_of(start, 8), WIN), :].astype(jnp.bfloat16),
                    inverse[...],
                    TN,
                    preferred_element_type=jnp.float32,
                ).astype(jnp.bfloat16)

            out_copy(group, slot).start()

    for slot in range(2):
        out_copy(6 + slot, slot).wait()


def correlate(sources, receivers, inverse):
    return pl.pallas_call(
        correlate_kernel,
        out_shape=jax.ShapeDtypeStruct((64, 128, WIN), jnp.bfloat16),
        in_specs=[pl.BlockSpec(memory_space=pltpu.VMEM)] * 2 + [pl.BlockSpec(memory_space=pltpu.HBM)],
        out_specs=pl.BlockSpec(memory_space=pl.ANY),
        scratch_shapes=[
            pltpu.VMEM((64 * PITCH, 128), jnp.float32),
            pltpu.VMEM((2, 8, 128, WIN), jnp.bfloat16),
            pltpu.VMEM((WIN, WIN), jnp.bfloat16),
            pltpu.SemaphoreType.DMA((3,)),
        ],
        compiler_params=pltpu.CompilerParams(vmem_limit_bytes=24 * 1024 * 1024),
        name="correlate",
    )(sources, receivers, inverse)


def local(raw_data, row_owner, source_blocks):
    sources, receivers = exchange(raw_data, row_owner, source_blocks)
    inverse = jnp.asarray(inverse_table(32), jnp.bfloat16)
    lagged = correlate(sources, receivers, inverse)
    return lagged.reshape(2, 32, 128, WIN)


def solution(mesh):
    placed = (P("seg", "recv", None), P("recv", None), P())
    return jax.shard_map(
        local, mesh=mesh, in_specs=placed, out_specs=P(None, "seg", "recv", None), check_vma=False
    )
```

```python
import functools
import math

import jax
import jax.numpy as jnp
import ml_dtypes
import numpy as np
from jax import lax
from jax.experimental import pallas as pl
from jax.experimental.pallas import tpu as pltpu
from jax.sharding import PartitionSpec as P

WIN = 512
NB = 128
HALF = 256
STEP = 72
PITCH = 520
NT = (((1,), (1,)), ((), ()))
TN = (((0,), (0,)), ((), ()))


def forward_table():
    sample, freq = np.arange(WIN), np.arange(HALF)
    angles = (sample[:, None] * freq[None, :] % WIN) * (2.0 * math.pi / WIN)
    parity = np.where(sample % 2 == 0, 1.0, -1.0)
    sines = np.where(freq[None, :] == 0, parity[:, None], -np.sin(angles))
    return np.concatenate([np.cos(angles), sines], axis=1)


def inverse_table(window_total):
    lag, freq = np.arange(WIN) - HALF, np.arange(HALF)
    angles = (freq[:, None] * lag[None, :] % WIN) * (2.0 * math.pi / WIN)
    factor = 1.0 / (WIN * math.sqrt(window_total * WIN))
    parity = np.where(lag % 2 == 0, 1.0, -1.0)
    zero = freq[:, None] == 0
    cosine_rows = np.where(zero, factor, 2.0 * factor * np.cos(angles))
    sine_rows = np.where(zero, factor * parity[None, :], -2.0 * factor * np.sin(angles))
    return np.concatenate([cosine_rows, sine_rows], axis=0)


def forward_halves():
    table = forward_table().astype(np.float32)
    high = table.astype(ml_dtypes.bfloat16)
    low = (table - high.astype(np.float32)).astype(ml_dtypes.bfloat16)
    return jnp.asarray(np.stack([high, low]))


ORDER = (2, 1, 3, 0)
GROUPS = ((0, 1), (1, 1), (2, 2))


def split(values):
    high = values.astype(jnp.bfloat16)
    return high, (values - high.astype(jnp.float32)).astype(jnp.bfloat16)


def product(left, right):
    return jnp.dot(left, right, preferred_element_type=jnp.float32)


def place_of(turn):
    place = 0
    for number, listed in enumerate(ORDER):
        place = place + number * (turn == listed).astype(jnp.int32)
    return place


def prepare(zh, blocks, raw, owner, table, slots, first, spectra):
    row = lax.broadcasted_iota(jnp.int32, (64, 512), 0)
    lane = lax.broadcasted_iota(jnp.int32, (64, 512), 1)
    diagonal = row[:, :64] == lane[:, :64]
    owner_column = jnp.sum(jnp.where(diagonal, owner[...], 0), axis=1, keepdims=True)
    owner_row = jnp.sum(jnp.where(row == lane % 64, owner_column, 0), axis=0, keepdims=True)
    same = (owner_column == owner_row) & (row < lane % 64)
    rank = jnp.sum(same.astype(jnp.int32), axis=0, keepdims=True)
    place = owner_row // 4 * 4 + place_of((owner_row % 4 + 4 - zh) % 4)
    target = (place * 2 + rank) * 8 + lax.broadcasted_iota(jnp.int32, (1, 512), 1) // 64
    for window in range(8):
        parts = []
        for run in range(4):
            start = (window % 4 * 4 + run) * NB
            values = raw[window // 4, :, start : start + NB]
            amplitude = jnp.mean(jnp.abs(values), axis=-1, keepdims=True) + 1e-06
            parts.append(values / amplitude)
        high, low = split(jnp.concatenate(parts, axis=1))
        spectra[window * 64 : window * 64 + 64, :] = (
            product(high, table[0]) + (product(low, table[0]) + product(high, table[1]))
        ).astype(jnp.bfloat16)

    @pl.loop(0, 4, unroll=2)
    def _(part):
        placed = lax.broadcasted_iota(jnp.int32, (256, 512), 0) + part * 256 == target
        slots[pl.ds(part * 4, 4)] = product(
            placed.astype(jnp.float32).astype(jnp.bfloat16), spectra[...]
        ).astype(jnp.bfloat16).reshape(4, 4, 16, WIN)

    for b in range(2):
        block = blocks[b]
        first[b * 16 : b * 16 + 16, :] = slots[block // 4, place_of((block % 4 + 4 - zh) % 4)]


MESH = pl.DeviceIdType.MESH


def exchange_kernel(blocks, raw, owner, table, sources, receivers, spectra, slots, first, held, panels, placed, turned, staged, chunk, turn_send, turn_recv, xy_send, xy_recv, z_send, z_recv, pair_send, pair_recv,
                    core_send, core_recv, pz_send, pz_recv, pxy_send, pxy_recv, local_sem):
    recv = lax.axis_index("recv")
    seg = lax.axis_index("seg")
    y, x, zh = recv // 16, (recv // 4) % 4, recv % 4
    zl, core = seg // 2, seg % 2
    plane = y * 4 + x

    def plane_peer(step):
        return ((y + step // 4) % 4) * 4 + (x + step % 4) % 4

    def xy_copy(group, step):
        target = plane_peer(step)
        start, count = GROUPS[group]
        places = pl.ds(start, count)
        return pltpu.make_async_remote_copy(
            src_ref=slots.at[target, places],
            dst_ref=staged.at[places, plane],
            send_sem=xy_send.at[group, step],
            recv_sem=xy_recv.at[group, step],
            device_id=(target * 4 + zh, seg),
            device_id_type=MESH,
        )

    near = (None, 0, 1 - zl, 1)

    def half_of(half):
        return pl.ds(half * 8, 8)

    def held_from(turn, low, owner_core, half):
        return held.at[low * 2 + owner_core, half_of(half), (zh + 4 - turn) % 4]

    def z_copy(turn, low, half):
        return pltpu.make_async_remote_copy(
            src_ref=staged.at[ORDER.index(turn), half_of(half)],
            dst_ref=held.at[seg, half_of(half), zh],
            send_sem=z_send.at[turn, half],
            recv_sem=z_recv.at[turn, zl, half],
            device_id=(plane * 4 + (zh + turn) % 4, low * 2 + core),
            device_id_type=MESH,
        )

    def z_arrival(turn, low, half):
        return pltpu.make_async_remote_copy(
            src_ref=staged.at[0, half_of(half)],
            dst_ref=held_from(turn, low, core, half),
            send_sem=z_send.at[turn, half],
            recv_sem=z_recv.at[turn, low, half],
            device_id=(recv, seg),
            device_id_type=MESH,
        )

    def pair_copy(turn, low, half):
        place = held_from(turn, low, core, half)
        return pltpu.make_async_remote_copy(
            src_ref=place,
            dst_ref=place,
            send_sem=pair_send.at[turn, low, half],
            recv_sem=pair_recv.at[turn, low, half],
            device_id=(recv, (1 - zl) * 2 + core),
            device_id_type=MESH,
        )

    def core_copy(turn, low, half):
        place = held_from(turn, low, core, half)
        return pltpu.make_async_remote_copy(
            src_ref=place,
            dst_ref=place,
            send_sem=core_send.at[turn, low, half],
            recv_sem=core_recv.at[turn, low, half],
            device_id=(recv, zl * 2 + 1 - core),
            device_id_type=MESH,
        )

    def core_arrival(turn, low, half):
        place = held_from(turn, low, 1 - core, half)
        return pltpu.make_async_remote_copy(
            src_ref=place,
            dst_ref=place,
            send_sem=core_send.at[turn, low, half],
            recv_sem=core_recv.at[turn, low, half],
            device_id=(recv, seg),
            device_id_type=MESH,
        )

    def pz_copy(turn):
        return pltpu.make_async_remote_copy(
            src_ref=chunk,
            dst_ref=panels.at[plane, zh],
            send_sem=pz_send.at[turn],
            recv_sem=pz_recv.at[turn],
            device_id=(plane * 4 + (zh + turn) % 4, seg),
            device_id_type=MESH,
        )

    def pxy_copy(step):
        return pltpu.make_async_remote_copy(
            src_ref=panels.at[plane],
            dst_ref=panels.at[plane],
            send_sem=pxy_send.at[step],
            recv_sem=pxy_recv.at[step],
            device_id=(plane_peer(step) * 4 + zh, seg),
            device_id_type=MESH,
        )

    def turn_copy():
        return pltpu.make_async_remote_copy(
            src_ref=first,
            dst_ref=chunk,
            send_sem=turn_send,
            recv_sem=turn_recv,
            device_id=((seg * 4 + x) * 4 + zh, y),
            device_id_type=MESH,
        )

    row = lax.broadcasted_iota(jnp.int32, (256, 256), 0)
    column = lax.broadcasted_iota(jnp.int32, (256, 256), 1)

    def zero_one(hits):
        return hits.astype(jnp.float32).astype(jnp.bfloat16)

    def place_block(window_group, block):
        order = zero_one(row % 32 // 2 * 16 + row % 2 * 8 + row // 32 == column)
        rows = jnp.dot(
            order,
            held[window_group, :, block].reshape(256, WIN),
            preferred_element_type=jnp.float32,
        ).astype(jnp.bfloat16)
        for w in range(8):
            start = (window_group * 8 + w) * 128 + block * 32
            placed[pl.ds(pl.multiple_of(start, 32), 32), :] = rows[w * 32 : w * 32 + 32]

    def turn_receivers():
        channel = row % 128
        order = zero_one(
            (column // 128 == row // 128)
            & (column % 128 == channel % 32 // 2 * 8 + channel // 32 * 2 + channel % 2)
        )

        @pl.loop(0, 16, unroll=4)
        def _(n):
            for c in range(2):
                block = placed[pl.ds(pl.multiple_of(n * 256, 256), 256), c * HALF : c * HALF + HALF]
                part = lax.dot_general(block, order, TN, preferred_element_type=jnp.float32)
                for w in range(2):
                    receivers[pl.ds(c * 32 + n * 2 + w, HALF, stride=STEP), :] = part[
                        :, w * 128 : w * 128 + 128
                    ]

    def turn_sources(window_group):
        order = zero_one(row % 16 // 2 * 32 + row % 32 // 16 * 16 + row % 2 * 8 + row // 32 == column)
        same = zero_one(row == column)
        low_lane = lax.broadcasted_iota(jnp.int32, (HALF, 128), 1) < 64
        zero_row = lax.broadcasted_iota(jnp.int32, (HALF, 128), 0) == 0
        for g in range(2):
            block = panels[pl.ds(window_group * 4 + g * 2, 2)].reshape(256, WIN)
            rows = jnp.dot(order, block, preferred_element_type=jnp.float32).astype(jnp.bfloat16)
            for w in range(8):
                for b in range(2):
                    for copy in range(2):
                        start = w * 128 + copy * 64 + b * 32 + g * 16
                        turned[start : start + 16, :] = rows[w * 32 + b * 16 : w * 32 + b * 16 + 16]
        for n in range(4):
            real, imag = (
                lax.dot_general(
                    same,
                    turned[n * 256 : n * 256 + 256, c * HALF : c * HALF + HALF],
                    NT,
                    preferred_element_type=jnp.float32,
                )
                for c in range(2)
            )
            for w in range(2):
                re, im = real[:, w * 128 : w * 128 + 128], imag[:, w * 128 : w * 128 + 128]
                window = window_group * 8 + n * 2 + w
                sources[pl.ds(window, HALF, stride=STEP), :] = jnp.where(
                    low_lane, re, jnp.where(zero_row, 0.0, -im)
                )
                sources[pl.ds(32 + window, HALF, stride=STEP), :] = jnp.where(
                    low_lane, jnp.where(zero_row, 0.0, im), jnp.where(zero_row, im, re)
                )

    barrier = pltpu.get_barrier_semaphore()

    @pl.when(y != seg)
    def _():
        pl.semaphore_signal(barrier, inc=1, device_id=((seg * 4 + x) * 4 + zh, y), device_id_type=MESH)

    @pl.loop(1, 16)
    def _(step):
        pl.semaphore_signal(barrier, inc=1, device_id=(plane_peer(step) * 4 + zh, seg), device_id_type=MESH)

    @pl.loop(1, 8)
    def _(step):
        z = (zh * 2 + zl + step) % 8
        pl.semaphore_signal(
            barrier, inc=1, device_id=(plane * 4 + z // 2, (z % 2) * 2 + core), device_id_type=MESH
        )

    pl.semaphore_signal(barrier, inc=1, device_id=(recv, zl * 2 + 1 - core), device_id_type=MESH)
    prepare(zh, blocks, raw, owner, table, slots, first, spectra)
    kept_chunk = pltpu.make_async_copy(first, chunk, local_sem.at[6])
    own_chunk = pltpu.make_async_copy(chunk, panels.at[plane, zh], local_sem.at[4])

    @pl.when(y == seg)
    def _():
        kept_chunk.start()

    own = pltpu.make_async_copy(slots.at[plane], staged.at[:, plane], local_sem.at[0])
    own.start()

    @pl.when(y == seg)
    def _():
        pl.semaphore_wait(barrier, 23)

    @pl.when(y != seg)
    def _():
        pl.semaphore_wait(barrier, 24)
        turn_copy().start()

    for group in range(len(GROUPS)):

        @pl.loop(1, 16)
        def _(step):
            xy_copy(group, step).start()

    @pl.when(y != seg)
    def _():
        turn_copy().wait()

    @pl.when(y == seg)
    def _():
        kept_chunk.wait()

    own_chunk.start()
    for turn in (1, 2, 3):
        pz_copy(turn).start()

    kept = pltpu.make_async_copy(staged.at[ORDER.index(0)], held.at[seg, :, zh], local_sem.at[5])
    own.wait()
    for group, (start, count) in enumerate(GROUPS):

        @pl.loop(1, 16)
        def _(step):
            xy_copy(group, step).wait_recv()

        for turn in ORDER[start : start + count]:
            for half in range(2):
                z_copy(turn, near[turn] if turn else 1 - zl, half).start()
            if not turn:
                kept.start()
        if group == 0:
            own_chunk.wait()
            for other in (1, 2, 3):
                pz_copy(other).wait_recv()

            @pl.loop(1, 16)
            def _(step):
                pxy_copy(step).start()

    kept.wait()
    for half in range(2):
        core_copy(0, zl, half).start()
    direct, far = 1 + 2 * zl, 3 - 2 * zl
    for turn, low in ((2, 1 - zl), (direct, 0), (direct, 1)):
        for half in range(2):
            z_arrival(turn, low, half).wait_recv()
            pair_copy(turn, low, half).start()
            core_copy(turn, low, half).start()
    for half in range(2):
        z_arrival(0, 1 - zl, half).wait_recv()
        core_copy(0, 1 - zl, half).start()

    early = ((0, zl), (2, 1 - zl), (direct, 0), (direct, 1), (0, 1 - zl))
    late = ((2, zl), (far, 0), (far, 1))
    for turn, low in early:
        place_block(low * 2 + core, (zh + 4 - turn) % 4)
    for turn, low in early:
        for half in range(2):
            core_arrival(turn, low, half).wait_recv()
        place_block(low * 2 + 1 - core, (zh + 4 - turn) % 4)

    @pl.loop(1, 16)
    def _(step):
        pxy_copy(step).wait_recv()

    @pl.loop(0, 4)
    def _(window_group):
        turn_sources(window_group)

    for turn, low in late:
        for half in range(2):
            pair_copy(turn, low, half).wait_recv()
            core_copy(turn, low, half).start()
        place_block(low * 2 + core, (zh + 4 - turn) % 4)
    for turn, low in late:
        for half in range(2):
            core_arrival(turn, low, half).wait_recv()
        place_block(low * 2 + 1 - core, (zh + 4 - turn) % 4)
    turn_receivers()

    @pl.loop(1, 16)
    def _(step):
        pxy_copy(step).wait_send()
        for group in range(len(GROUPS)):
            xy_copy(group, step).wait_send()

    for turn in (1, 2, 3):
        pz_copy(turn).wait_send()
    for half in range(2):
        for turn in range(4):
            z_copy(turn, near[turn] if turn else 1 - zl, half).wait_send()
            for low in (0, 1):
                core_copy(turn, low, half).wait_send()
        for turn, low in ((2, 1 - zl), (direct, 0), (direct, 1)):
            pair_copy(turn, low, half).wait_send()


def exchange(raw_data, row_owner, source_blocks):
    dma = pltpu.SemaphoreType.DMA
    bf16 = jnp.bfloat16
    return pl.pallas_call(
        exchange_kernel,
        out_shape=(
            jax.ShapeDtypeStruct((HALF * STEP, 128), jnp.float32),
            jax.ShapeDtypeStruct((HALF * STEP, 128), jnp.float32),
        ),
        in_specs=[pl.BlockSpec(memory_space=pltpu.SMEM)] + [pl.BlockSpec(memory_space=pltpu.VMEM)] * 3,
        out_specs=(pl.BlockSpec(memory_space=pltpu.VMEM),) * 2,
        scratch_shapes=[
            pltpu.VMEM((512, WIN), bf16),
            pltpu.VMEM((16, 4, 16, WIN), bf16),
            pltpu.VMEM((32, WIN), bf16),
            pltpu.VMEM((4, 16, 4, 16, WIN), bf16),
            pltpu.VMEM((16, 4, 32, WIN), bf16),
            pltpu.VMEM((4096, WIN), bf16),
            pltpu.VMEM((1024, WIN), bf16),
            pltpu.VMEM((4, 16, 16, WIN), bf16),
            pltpu.VMEM((32, WIN), bf16),
            dma, dma, dma((4, 16)), dma((4, 16)), dma((4, 2)), dma((4, 2, 2)),
            dma((4, 2, 2)), dma((4, 2, 2)), dma((4, 2, 2)), dma((4, 2, 2)),
            dma((4,)), dma((4,)), dma((16,)), dma((16,)), dma((7,)),
        ],
        compiler_params=pltpu.CompilerParams(
            collective_id=0, has_side_effects=True, vmem_limit_bytes=24576 * 1024
        ),
        name="exchange",
    )(source_blocks, raw_data, row_owner.reshape(1, 64), forward_halves())


def correlate_kernel(sources, receivers, inverse_hbm, out, stack, lagged, inverse, sent):
    table_copy = pltpu.make_async_copy(inverse_hbm, inverse, sent.at[2])
    table_copy.start()

    @pl.loop(0, HALF, unroll=64)
    def _(j):
        at = pl.ds(pl.multiple_of(j * STEP, 8), 64)
        terms = lax.dot_general(
            sources[at, :].astype(jnp.bfloat16),
            receivers[at, :].astype(jnp.bfloat16),
            TN,
            preferred_element_type=jnp.float32,
        )
        stack[pl.ds(j, 64, stride=PITCH), :] = terms[:64]
        stack[pl.ds(HALF + j, 64, stride=PITCH), :] = terms[64:]

    def out_copy(group, slot):
        return pltpu.make_async_copy(lagged.at[slot], out.at[pl.ds(group * 8, 8)], sent.at[slot])

    table_copy.wait()

    @pl.loop(0, 4)
    def _(pair):
        for slot in range(2):
            group = pair * 2 + slot

            @pl.when(pair > 0)
            def _():
                out_copy(group - 2, slot).wait()

            @pl.loop(0, 8, unroll=8)
            def _(i):
                start = (group * 8 + i) * PITCH
                lagged[slot, i] = lax.dot_general(
                    stack[pl.ds(pl.multiple_of(start, 8), WIN), :].astype(jnp.bfloat16),
                    inverse[...],
                    TN,
                    preferred_element_type=jnp.float32,
                ).astype(jnp.bfloat16)

            out_copy(group, slot).start()

    for slot in range(2):
        out_copy(6 + slot, slot).wait()


def correlate(sources, receivers, inverse):
    return pl.pallas_call(
        correlate_kernel,
        out_shape=jax.ShapeDtypeStruct((64, 128, WIN), jnp.bfloat16),
        in_specs=[pl.BlockSpec(memory_space=pltpu.VMEM)] * 2 + [pl.BlockSpec(memory_space=pltpu.HBM)],
        out_specs=pl.BlockSpec(memory_space=pl.ANY),
        scratch_shapes=[
            pltpu.VMEM((64 * PITCH, 128), jnp.float32),
            pltpu.VMEM((2, 8, 128, WIN), jnp.bfloat16),
            pltpu.VMEM((WIN, WIN), jnp.bfloat16),
            pltpu.SemaphoreType.DMA((3,)),
        ],
        compiler_params=pltpu.CompilerParams(vmem_limit_bytes=24 * 1024 * 1024),
        name="correlate",
    )(sources, receivers, inverse)


def local(raw_data, row_owner, source_blocks):
    sources, receivers = exchange(raw_data, row_owner, source_blocks)
    inverse = jnp.asarray(inverse_table(32), jnp.bfloat16)
    lagged = correlate(sources, receivers, inverse)
    return lagged.reshape(2, 32, 128, WIN)


def solution(mesh):
    placed = (P("seg", "recv", None), P("recv", None), P())
    return jax.shard_map(
        local, mesh=mesh, in_specs=placed, out_specs=P(None, "seg", "recv", None), check_vma=False
    )
```

```python
import functools
import math

import jax
import jax.numpy as jnp
import ml_dtypes
import numpy as np
from jax import lax
from jax.experimental import pallas as pl
from jax.experimental.pallas import tpu as pltpu
from jax.sharding import PartitionSpec as P

WIN = 512
NB = 128
HALF = 256
STEP = 72
PITCH = 520
NT = (((1,), (1,)), ((), ()))
TN = (((0,), (0,)), ((), ()))


def forward_table():
    sample, freq = np.arange(WIN), np.arange(HALF)
    angles = (sample[:, None] * freq[None, :] % WIN) * (2.0 * math.pi / WIN)
    parity = np.where(sample % 2 == 0, 1.0, -1.0)
    sines = np.where(freq[None, :] == 0, parity[:, None], -np.sin(angles))
    return np.concatenate([np.cos(angles), sines], axis=1)


def forward_halves():
    table = forward_table().astype(np.float32)
    high = table.astype(ml_dtypes.bfloat16)
    low = (table - high.astype(np.float32)).astype(ml_dtypes.bfloat16)
    return jnp.asarray(np.stack([high, low]))


ORDER = (2, 1, 3, 0)
GROUPS = ((0, 1), (1, 1), (2, 2))


def split(values):
    high = values.astype(jnp.bfloat16)
    return high, (values - high.astype(jnp.float32)).astype(jnp.bfloat16)


def product(left, right):
    return jnp.dot(left, right, preferred_element_type=jnp.float32)


def place_of(turn):
    place = 0
    for number, listed in enumerate(ORDER):
        place = place + number * (turn == listed).astype(jnp.int32)
    return place


def prepare(zh, blocks, raw, owner, table, slots, first, spectra):
    row = lax.broadcasted_iota(jnp.int32, (64, 512), 0)
    lane = lax.broadcasted_iota(jnp.int32, (64, 512), 1)
    diagonal = row[:, :64] == lane[:, :64]
    owner_column = jnp.sum(jnp.where(diagonal, owner[...], 0), axis=1, keepdims=True)
    owner_row = jnp.sum(jnp.where(row == lane % 64, owner_column, 0), axis=0, keepdims=True)
    same = (owner_column == owner_row) & (row < lane % 64)
    rank = jnp.sum(same.astype(jnp.int32), axis=0, keepdims=True)
    place = owner_row // 4 * 4 + place_of((owner_row % 4 + 4 - zh) % 4)
    target = (place * 2 + rank) * 8 + lax.broadcasted_iota(jnp.int32, (1, 512), 1) // 64
    for window in range(8):
        parts = []
        for run in range(4):
            start = (window % 4 * 4 + run) * NB
            values = raw[window // 4, :, start : start + NB]
            amplitude = jnp.mean(jnp.abs(values), axis=-1, keepdims=True) + 1e-06
            parts.append(values / amplitude)
        high, low = split(jnp.concatenate(parts, axis=1))
        spectra[window * 64 : window * 64 + 64, :] = (
            product(high, table[0]) + (product(low, table[0]) + product(high, table[1]))
        ).astype(jnp.bfloat16)

    @pl.loop(0, 4, unroll=2)
    def _(part):
        placed = lax.broadcasted_iota(jnp.int32, (256, 512), 0) + part * 256 == target
        slots[pl.ds(part * 4, 4)] = product(
            placed.astype(jnp.float32).astype(jnp.bfloat16), spectra[...]
        ).astype(jnp.bfloat16).reshape(4, 4, 16, WIN)

    for b in range(2):
        block = blocks[b]
        first[b * 16 : b * 16 + 16, :] = slots[block // 4, place_of((block % 4 + 4 - zh) % 4)]


MESH = pl.DeviceIdType.MESH


def exchange_kernel(blocks, raw, owner, table, sources, receivers, inverse, spectra, slots, first, held, panels, placed, turned, staged, chunk, turn_send, turn_recv, xy_send, xy_recv, z_send, z_recv, pair_send, pair_recv,
                    core_send, core_recv, pz_send, pz_recv, pxy_send, pxy_recv, local_sem):
    recv = lax.axis_index("recv")
    seg = lax.axis_index("seg")
    y, x, zh = recv // 16, (recv // 4) % 4, recv % 4
    zl, core = seg // 2, seg % 2
    plane = y * 4 + x

    def plane_peer(step):
        return ((y + step // 4) % 4) * 4 + (x + step % 4) % 4

    def xy_copy(group, step):
        target = plane_peer(step)
        start, count = GROUPS[group]
        places = pl.ds(start, count)
        return pltpu.make_async_remote_copy(
            src_ref=slots.at[target, places],
            dst_ref=staged.at[places, plane],
            send_sem=xy_send.at[group, step],
            recv_sem=xy_recv.at[group, step],
            device_id=(target * 4 + zh, seg),
            device_id_type=MESH,
        )

    near = (None, 0, 1 - zl, 1)

    def half_of(half):
        return pl.ds(half * 8, 8)

    def held_from(turn, low, owner_core, half):
        return held.at[low * 2 + owner_core, half_of(half), (zh + 4 - turn) % 4]

    def z_copy(turn, low, half):
        return pltpu.make_async_remote_copy(
            src_ref=staged.at[ORDER.index(turn), half_of(half)],
            dst_ref=held.at[seg, half_of(half), zh],
            send_sem=z_send.at[turn, half],
            recv_sem=z_recv.at[turn, zl, half],
            device_id=(plane * 4 + (zh + turn) % 4, low * 2 + core),
            device_id_type=MESH,
        )

    def z_arrival(turn, low, half):
        return pltpu.make_async_remote_copy(
            src_ref=staged.at[0, half_of(half)],
            dst_ref=held_from(turn, low, core, half),
            send_sem=z_send.at[turn, half],
            recv_sem=z_recv.at[turn, low, half],
            device_id=(recv, seg),
            device_id_type=MESH,
        )

    def pair_copy(turn, low, half):
        place = held_from(turn, low, core, half)
        return pltpu.make_async_remote_copy(
            src_ref=place,
            dst_ref=place,
            send_sem=pair_send.at[turn, low, half],
            recv_sem=pair_recv.at[turn, low, half],
            device_id=(recv, (1 - zl) * 2 + core),
            device_id_type=MESH,
        )

    def core_copy(turn, low, half):
        place = held_from(turn, low, core, half)
        return pltpu.make_async_remote_copy(
            src_ref=place,
            dst_ref=place,
            send_sem=core_send.at[turn, low, half],
            recv_sem=core_recv.at[turn, low, half],
            device_id=(recv, zl * 2 + 1 - core),
            device_id_type=MESH,
        )

    def core_arrival(turn, low, half):
        place = held_from(turn, low, 1 - core, half)
        return pltpu.make_async_remote_copy(
            src_ref=place,
            dst_ref=place,
            send_sem=core_send.at[turn, low, half],
            recv_sem=core_recv.at[turn, low, half],
            device_id=(recv, seg),
            device_id_type=MESH,
        )

    def pz_copy(turn):
        return pltpu.make_async_remote_copy(
            src_ref=chunk,
            dst_ref=panels.at[plane, zh],
            send_sem=pz_send.at[turn],
            recv_sem=pz_recv.at[turn],
            device_id=(plane * 4 + (zh + turn) % 4, seg),
            device_id_type=MESH,
        )

    def pxy_copy(step):
        return pltpu.make_async_remote_copy(
            src_ref=panels.at[plane],
            dst_ref=panels.at[plane],
            send_sem=pxy_send.at[step],
            recv_sem=pxy_recv.at[step],
            device_id=(plane_peer(step) * 4 + zh, seg),
            device_id_type=MESH,
        )

    def turn_copy():
        return pltpu.make_async_remote_copy(
            src_ref=first,
            dst_ref=chunk,
            send_sem=turn_send,
            recv_sem=turn_recv,
            device_id=((seg * 4 + x) * 4 + zh, y),
            device_id_type=MESH,
        )

    row = lax.broadcasted_iota(jnp.int32, (256, 256), 0)
    column = lax.broadcasted_iota(jnp.int32, (256, 256), 1)

    def zero_one(hits):
        return hits.astype(jnp.float32).astype(jnp.bfloat16)

    def place_block(window_group, block):
        order = zero_one(row % 32 // 2 * 16 + row % 2 * 8 + row // 32 == column)
        rows = jnp.dot(
            order,
            held[window_group, :, block].reshape(256, WIN),
            preferred_element_type=jnp.float32,
        ).astype(jnp.bfloat16)
        for w in range(8):
            start = (window_group * 8 + w) * 128 + block * 32
            placed[pl.ds(pl.multiple_of(start, 32), 32), :] = rows[w * 32 : w * 32 + 32]

    def turn_receivers():
        channel = row % 128
        order = zero_one(
            (column // 128 == row // 128)
            & (column % 128 == channel % 32 // 2 * 8 + channel // 32 * 2 + channel % 2)
        )

        @pl.loop(0, 16, unroll=4)
        def _(n):
            for c in range(2):
                block = placed[pl.ds(pl.multiple_of(n * 256, 256), 256), c * HALF : c * HALF + HALF]
                part = lax.dot_general(block, order, TN, preferred_element_type=jnp.float32)
                for w in range(2):
                    receivers[pl.ds(c * 32 + n * 2 + w, HALF, stride=STEP), :] = part[
                        :, w * 128 : w * 128 + 128
                    ]

    def turn_table():
        same = zero_one(row == column)
        scale = 1.0 / (WIN * math.sqrt(32 * WIN))
        factor = jnp.where(row == 0, scale, 2.0 * scale * (1 - 2 * (row % 2)).astype(jnp.float32))
        for c in range(2):
            for d in range(2):
                part = lax.dot_general(
                    same,
                    table[0, d * HALF : d * HALF + HALF, c * HALF : c * HALF + HALF],
                    NT,
                    preferred_element_type=jnp.float32,
                )
                inverse[c * HALF : c * HALF + HALF, d * HALF : d * HALF + HALF] = (
                    part * factor
                ).astype(jnp.bfloat16)

    def turn_sources(window_group):
        order = zero_one(row % 16 // 2 * 32 + row % 32 // 16 * 16 + row % 2 * 8 + row // 32 == column)
        same = zero_one(row == column)
        low_lane = lax.broadcasted_iota(jnp.int32, (HALF, 128), 1) < 64
        zero_row = lax.broadcasted_iota(jnp.int32, (HALF, 128), 0) == 0
        for g in range(2):
            block = panels[pl.ds(window_group * 4 + g * 2, 2)].reshape(256, WIN)
            rows = jnp.dot(order, block, preferred_element_type=jnp.float32).astype(jnp.bfloat16)
            for w in range(8):
                for b in range(2):
                    for copy in range(2):
                        start = w * 128 + copy * 64 + b * 32 + g * 16
                        turned[start : start + 16, :] = rows[w * 32 + b * 16 : w * 32 + b * 16 + 16]
        for n in range(4):
            real, imag = (
                lax.dot_general(
                    same,
                    turned[n * 256 : n * 256 + 256, c * HALF : c * HALF + HALF],
                    NT,
                    preferred_element_type=jnp.float32,
                )
                for c in range(2)
            )
            for w in range(2):
                re, im = real[:, w * 128 : w * 128 + 128], imag[:, w * 128 : w * 128 + 128]
                window = window_group * 8 + n * 2 + w
                sources[pl.ds(window, HALF, stride=STEP), :] = jnp.where(
                    low_lane, re, jnp.where(zero_row, 0.0, -im)
                )
                sources[pl.ds(32 + window, HALF, stride=STEP), :] = jnp.where(
                    low_lane, jnp.where(zero_row, 0.0, im), jnp.where(zero_row, im, re)
                )

    barrier = pltpu.get_barrier_semaphore()

    @pl.when(y != seg)
    def _():
        pl.semaphore_signal(barrier, inc=1, device_id=((seg * 4 + x) * 4 + zh, y), device_id_type=MESH)

    @pl.loop(1, 16)
    def _(step):
        pl.semaphore_signal(barrier, inc=1, device_id=(plane_peer(step) * 4 + zh, seg), device_id_type=MESH)

    @pl.loop(1, 8)
    def _(step):
        z = (zh * 2 + zl + step) % 8
        pl.semaphore_signal(
            barrier, inc=1, device_id=(plane * 4 + z // 2, (z % 2) * 2 + core), device_id_type=MESH
        )

    pl.semaphore_signal(barrier, inc=1, device_id=(recv, zl * 2 + 1 - core), device_id_type=MESH)
    prepare(zh, blocks, raw, owner, table, slots, first, spectra)
    kept_chunk = pltpu.make_async_copy(first, chunk, local_sem.at[6])
    own_chunk = pltpu.make_async_copy(chunk, panels.at[plane, zh], local_sem.at[4])

    @pl.when(y == seg)
    def _():
        kept_chunk.start()

    own = pltpu.make_async_copy(slots.at[plane], staged.at[:, plane], local_sem.at[0])
    own.start()

    @pl.when(y == seg)
    def _():
        pl.semaphore_wait(barrier, 23)

    @pl.when(y != seg)
    def _():
        pl.semaphore_wait(barrier, 24)
        turn_copy().start()

    for group in range(len(GROUPS)):

        @pl.loop(1, 16)
        def _(step):
            xy_copy(group, step).start()

    @pl.when(y != seg)
    def _():
        turn_copy().wait()

    @pl.when(y == seg)
    def _():
        kept_chunk.wait()

    own_chunk.start()
    for turn in (1, 2, 3):
        pz_copy(turn).start()

    kept = pltpu.make_async_copy(staged.at[ORDER.index(0)], held.at[seg, :, zh], local_sem.at[5])
    own.wait()
    for group, (start, count) in enumerate(GROUPS):

        @pl.loop(1, 16)
        def _(step):
            xy_copy(group, step).wait_recv()

        for turn in ORDER[start : start + count]:
            for half in range(2):
                z_copy(turn, near[turn] if turn else 1 - zl, half).start()
            if not turn:
                kept.start()
        if group == 0:
            own_chunk.wait()
            for other in (1, 2, 3):
                pz_copy(other).wait_recv()

            @pl.loop(1, 16)
            def _(step):
                pxy_copy(step).start()

    kept.wait()
    for half in range(2):
        core_copy(0, zl, half).start()
    direct, far = 1 + 2 * zl, 3 - 2 * zl
    for turn, low in ((2, 1 - zl), (direct, 0), (direct, 1)):
        for half in range(2):
            z_arrival(turn, low, half).wait_recv()
            pair_copy(turn, low, half).start()
            core_copy(turn, low, half).start()
    for half in range(2):
        z_arrival(0, 1 - zl, half).wait_recv()
        core_copy(0, 1 - zl, half).start()

    early = ((0, zl), (2, 1 - zl), (direct, 0), (direct, 1), (0, 1 - zl))
    late = ((2, zl), (far, 0), (far, 1))
    for turn, low in early:
        place_block(low * 2 + core, (zh + 4 - turn) % 4)
    for turn, low in early:
        for half in range(2):
            core_arrival(turn, low, half).wait_recv()
        place_block(low * 2 + 1 - core, (zh + 4 - turn) % 4)

    turn_table()

    @pl.loop(1, 16)
    def _(step):
        pxy_copy(step).wait_recv()

    @pl.loop(0, 4)
    def _(window_group):
        turn_sources(window_group)

    for turn, low in late:
        for half in range(2):
            pair_copy(turn, low, half).wait_recv()
            core_copy(turn, low, half).start()
        place_block(low * 2 + core, (zh + 4 - turn) % 4)
    for turn, low in late:
        for half in range(2):
            core_arrival(turn, low, half).wait_recv()
        place_block(low * 2 + 1 - core, (zh + 4 - turn) % 4)
    turn_receivers()

    @pl.loop(1, 16)
    def _(step):
        pxy_copy(step).wait_send()
        for group in range(len(GROUPS)):
            xy_copy(group, step).wait_send()

    for turn in (1, 2, 3):
        pz_copy(turn).wait_send()
    for half in range(2):
        for turn in range(4):
            z_copy(turn, near[turn] if turn else 1 - zl, half).wait_send()
            for low in (0, 1):
                core_copy(turn, low, half).wait_send()
        for turn, low in ((2, 1 - zl), (direct, 0), (direct, 1)):
            pair_copy(turn, low, half).wait_send()


def exchange(raw_data, row_owner, source_blocks):
    dma = pltpu.SemaphoreType.DMA
    bf16 = jnp.bfloat16
    return pl.pallas_call(
        exchange_kernel,
        out_shape=(
            jax.ShapeDtypeStruct((HALF * STEP, 128), jnp.float32),
            jax.ShapeDtypeStruct((HALF * STEP, 128), jnp.float32),
            jax.ShapeDtypeStruct((WIN, WIN), jnp.bfloat16),
        ),
        in_specs=[pl.BlockSpec(memory_space=pltpu.SMEM)] + [pl.BlockSpec(memory_space=pltpu.VMEM)] * 3,
        out_specs=(pl.BlockSpec(memory_space=pltpu.VMEM),) * 3,
        scratch_shapes=[
            pltpu.VMEM((512, WIN), bf16),
            pltpu.VMEM((16, 4, 16, WIN), bf16),
            pltpu.VMEM((32, WIN), bf16),
            pltpu.VMEM((4, 16, 4, 16, WIN), bf16),
            pltpu.VMEM((16, 4, 32, WIN), bf16),
            pltpu.VMEM((4096, WIN), bf16),
            pltpu.VMEM((1024, WIN), bf16),
            pltpu.VMEM((4, 16, 16, WIN), bf16),
            pltpu.VMEM((32, WIN), bf16),
            dma, dma, dma((4, 16)), dma((4, 16)), dma((4, 2)), dma((4, 2, 2)),
            dma((4, 2, 2)), dma((4, 2, 2)), dma((4, 2, 2)), dma((4, 2, 2)),
            dma((4,)), dma((4,)), dma((16,)), dma((16,)), dma((7,)),
        ],
        compiler_params=pltpu.CompilerParams(
            collective_id=0, has_side_effects=True, vmem_limit_bytes=24576 * 1024
        ),
        name="exchange",
    )(source_blocks, raw_data, row_owner.reshape(1, 64), forward_halves())


def correlate_kernel(sources, receivers, inverse, out, stack, lagged, sent):
    @pl.loop(0, HALF, unroll=64)
    def _(j):
        at = pl.ds(pl.multiple_of(j * STEP, 8), 64)
        terms = lax.dot_general(
            sources[at, :].astype(jnp.bfloat16),
            receivers[at, :].astype(jnp.bfloat16),
            TN,
            preferred_element_type=jnp.float32,
        )
        stack[pl.ds(j, 64, stride=PITCH), :] = terms[:64]
        stack[pl.ds(HALF + j, 64, stride=PITCH), :] = terms[64:]

    def out_copy(group, slot):
        return pltpu.make_async_copy(lagged.at[slot], out.at[pl.ds(group * 8, 8)], sent.at[slot])

    @pl.loop(0, 4)
    def _(pair):
        for slot in range(2):
            group = pair * 2 + slot

            @pl.when(pair > 0)
            def _():
                out_copy(group - 2, slot).wait()

            @pl.loop(0, 8, unroll=8)
            def _(i):
                start = (group * 8 + i) * PITCH
                lagged[slot, i] = lax.dot_general(
                    stack[pl.ds(pl.multiple_of(start, 8), WIN), :].astype(jnp.bfloat16),
                    inverse[...],
                    TN,
                    preferred_element_type=jnp.float32,
                ).astype(jnp.bfloat16)

            out_copy(group, slot).start()

    for slot in range(2):
        out_copy(6 + slot, slot).wait()


def correlate(sources, receivers, inverse):
    return pl.pallas_call(
        correlate_kernel,
        out_shape=jax.ShapeDtypeStruct((64, 128, WIN), jnp.bfloat16),
        in_specs=[pl.BlockSpec(memory_space=pltpu.VMEM)] * 3,
        out_specs=pl.BlockSpec(memory_space=pl.ANY),
        scratch_shapes=[
            pltpu.VMEM((64 * PITCH, 128), jnp.float32),
            pltpu.VMEM((2, 8, 128, WIN), jnp.bfloat16),
            pltpu.SemaphoreType.DMA((2,)),
        ],
        compiler_params=pltpu.CompilerParams(vmem_limit_bytes=24 * 1024 * 1024),
        name="correlate",
    )(sources, receivers, inverse)


def local(raw_data, row_owner, source_blocks):
    sources, receivers, inverse = exchange(raw_data, row_owner, source_blocks)
    lagged = correlate(sources, receivers, inverse)
    return lagged.reshape(2, 32, 128, WIN)


def solution(mesh):
    placed = (P("seg", "recv", None), P("recv", None), P())
    return jax.shard_map(
        local, mesh=mesh, in_specs=placed, out_specs=P(None, "seg", "recv", None), check_vma=False
    )
```

```python
import functools
import math

import jax
import jax.numpy as jnp
import ml_dtypes
import numpy as np
from jax import lax
from jax.experimental import pallas as pl
from jax.experimental.pallas import tpu as pltpu
from jax.sharding import PartitionSpec as P

WIN = 512
NB = 128
HALF = 256
STEP = 72
PITCH = 520
NT = (((1,), (1,)), ((), ()))
TN = (((0,), (0,)), ((), ()))


def forward_table():
    sample, freq = np.arange(WIN), np.arange(HALF)
    angles = (sample[:, None] * freq[None, :] % WIN) * (2.0 * math.pi / WIN)
    parity = np.where(sample % 2 == 0, 1.0, -1.0)
    sines = np.where(freq[None, :] == 0, parity[:, None], -np.sin(angles))
    return np.concatenate([np.cos(angles), sines], axis=1)


def forward_halves():
    table = forward_table().astype(np.float32)
    high = table.astype(ml_dtypes.bfloat16)
    low = (table - high.astype(np.float32)).astype(ml_dtypes.bfloat16)
    return jnp.asarray(np.stack([high, low]))


ORDER = (2, 1, 3, 0)
GROUPS = ((0, 1), (1, 1), (2, 2))


def split(values):
    high = values.astype(jnp.bfloat16)
    return high, (values - high.astype(jnp.float32)).astype(jnp.bfloat16)


def product(left, right):
    return jnp.dot(left, right, preferred_element_type=jnp.float32)


def place_of(turn):
    place = 0
    for number, listed in enumerate(ORDER):
        place = place + number * (turn == listed).astype(jnp.int32)
    return place


def prepare(zh, blocks, raw, owner, table, slots, first, spectra):
    row = lax.broadcasted_iota(jnp.int32, (64, 512), 0)
    lane = lax.broadcasted_iota(jnp.int32, (64, 512), 1)
    diagonal = row[:, :64] == lane[:, :64]
    owner_column = jnp.sum(jnp.where(diagonal, owner[...], 0), axis=1, keepdims=True)
    owner_row = jnp.sum(jnp.where(row == lane % 64, owner_column, 0), axis=0, keepdims=True)
    same = (owner_column == owner_row) & (row < lane % 64)
    rank = jnp.sum(same.astype(jnp.int32), axis=0, keepdims=True)
    place = owner_row // 4 * 4 + place_of((owner_row % 4 + 4 - zh) % 4)
    target = (place * 2 + rank) * 8 + lax.broadcasted_iota(jnp.int32, (1, 512), 1) // 64
    for window in range(8):
        parts = []
        for run in range(4):
            start = (window % 4 * 4 + run) * NB
            values = raw[window // 4, :, start : start + NB]
            amplitude = jnp.mean(jnp.abs(values), axis=-1, keepdims=True) + 1e-06
            parts.append(values / amplitude)
        high, low = split(jnp.concatenate(parts, axis=1))
        spectra[window * 64 : window * 64 + 64, :] = (
            product(high, table[0]) + (product(low, table[0]) + product(high, table[1]))
        ).astype(jnp.bfloat16)

    @pl.loop(0, 4, unroll=4)
    def _(part):
        placed = lax.broadcasted_iota(jnp.int32, (256, 512), 0) + part * 256 == target
        slots[pl.ds(part * 4, 4)] = product(
            placed.astype(jnp.float32).astype(jnp.bfloat16), spectra[...]
        ).astype(jnp.bfloat16).reshape(4, 4, 16, WIN)

    for b in range(2):
        block = blocks[b]
        first[b * 16 : b * 16 + 16, :] = slots[block // 4, place_of((block % 4 + 4 - zh) % 4)]


MESH = pl.DeviceIdType.MESH


def exchange_kernel(blocks, raw, owner, table, sources, receivers, inverse, spectra, slots, first, held, panels, placed, turned, staged, chunk, turn_send, turn_recv, xy_send, xy_recv, z_send, z_recv, pair_send, pair_recv,
                    core_send, core_recv, pz_send, pz_recv, pxy_send, pxy_recv, local_sem):
    recv = lax.axis_index("recv")
    seg = lax.axis_index("seg")
    y, x, zh = recv // 16, (recv // 4) % 4, recv % 4
    zl, core = seg // 2, seg % 2
    plane = y * 4 + x

    def plane_peer(step):
        return ((y + step // 4) % 4) * 4 + (x + step % 4) % 4

    def xy_copy(group, step):
        target = plane_peer(step)
        start, count = GROUPS[group]
        places = pl.ds(start, count)
        return pltpu.make_async_remote_copy(
            src_ref=slots.at[target, places],
            dst_ref=staged.at[places, plane],
            send_sem=xy_send.at[group, step],
            recv_sem=xy_recv.at[group, step],
            device_id=(target * 4 + zh, seg),
            device_id_type=MESH,
        )

    near = (None, 0, 1 - zl, 1)

    def half_of(half):
        return pl.ds(half * 8, 8)

    def held_from(turn, low, owner_core, half):
        return held.at[low * 2 + owner_core, half_of(half), (zh + 4 - turn) % 4]

    def z_copy(turn, low, half):
        return pltpu.make_async_remote_copy(
            src_ref=staged.at[ORDER.index(turn), half_of(half)],
            dst_ref=held.at[seg, half_of(half), zh],
            send_sem=z_send.at[turn, half],
            recv_sem=z_recv.at[turn, zl, half],
            device_id=(plane * 4 + (zh + turn) % 4, low * 2 + core),
            device_id_type=MESH,
        )

    def z_arrival(turn, low, half):
        return pltpu.make_async_remote_copy(
            src_ref=staged.at[0, half_of(half)],
            dst_ref=held_from(turn, low, core, half),
            send_sem=z_send.at[turn, half],
            recv_sem=z_recv.at[turn, low, half],
            device_id=(recv, seg),
            device_id_type=MESH,
        )

    def pair_copy(turn, low, half):
        place = held_from(turn, low, core, half)
        return pltpu.make_async_remote_copy(
            src_ref=place,
            dst_ref=place,
            send_sem=pair_send.at[turn, low, half],
            recv_sem=pair_recv.at[turn, low, half],
            device_id=(recv, (1 - zl) * 2 + core),
            device_id_type=MESH,
        )

    def core_copy(turn, low, half):
        place = held_from(turn, low, core, half)
        return pltpu.make_async_remote_copy(
            src_ref=place,
            dst_ref=place,
            send_sem=core_send.at[turn, low, half],
            recv_sem=core_recv.at[turn, low, half],
            device_id=(recv, zl * 2 + 1 - core),
            device_id_type=MESH,
        )

    def core_arrival(turn, low, half):
        place = held_from(turn, low, 1 - core, half)
        return pltpu.make_async_remote_copy(
            src_ref=place,
            dst_ref=place,
            send_sem=core_send.at[turn, low, half],
            recv_sem=core_recv.at[turn, low, half],
            device_id=(recv, seg),
            device_id_type=MESH,
        )

    def pz_copy(turn):
        return pltpu.make_async_remote_copy(
            src_ref=chunk,
            dst_ref=panels.at[plane, zh],
            send_sem=pz_send.at[turn],
            recv_sem=pz_recv.at[turn],
            device_id=(plane * 4 + (zh + turn) % 4, seg),
            device_id_type=MESH,
        )

    def pxy_copy(step):
        return pltpu.make_async_remote_copy(
            src_ref=panels.at[plane],
            dst_ref=panels.at[plane],
            send_sem=pxy_send.at[step],
            recv_sem=pxy_recv.at[step],
            device_id=(plane_peer(step) * 4 + zh, seg),
            device_id_type=MESH,
        )

    def turn_copy():
        return pltpu.make_async_remote_copy(
            src_ref=first,
            dst_ref=chunk,
            send_sem=turn_send,
            recv_sem=turn_recv,
            device_id=((seg * 4 + x) * 4 + zh, y),
            device_id_type=MESH,
        )

    row = lax.broadcasted_iota(jnp.int32, (256, 256), 0)
    column = lax.broadcasted_iota(jnp.int32, (256, 256), 1)

    def zero_one(hits):
        return hits.astype(jnp.float32).astype(jnp.bfloat16)

    def place_block(window_group, block):
        order = zero_one(row % 32 // 2 * 16 + row % 2 * 8 + row // 32 == column)
        rows = jnp.dot(
            order,
            held[window_group, :, block].reshape(256, WIN),
            preferred_element_type=jnp.float32,
        ).astype(jnp.bfloat16)
        for w in range(8):
            start = (window_group * 8 + w) * 128 + block * 32
            placed[pl.ds(pl.multiple_of(start, 32), 32), :] = rows[w * 32 : w * 32 + 32]

    def turn_receivers():
        channel = row % 128
        order = zero_one(
            (column // 128 == row // 128)
            & (column % 128 == channel % 32 // 2 * 8 + channel // 32 * 2 + channel % 2)
        )

        @pl.loop(0, 16, unroll=8)
        def _(n):
            for c in range(2):
                block = placed[pl.ds(pl.multiple_of(n * 256, 256), 256), c * HALF : c * HALF + HALF]
                part = lax.dot_general(block, order, TN, preferred_element_type=jnp.float32)
                for w in range(2):
                    receivers[pl.ds(c * 32 + n * 2 + w, HALF, stride=STEP), :] = part[
                        :, w * 128 : w * 128 + 128
                    ]

    def turn_table():
        same = zero_one(row == column)
        scale = 1.0 / (WIN * math.sqrt(32 * WIN))
        factor = jnp.where(row == 0, scale, 2.0 * scale * (1 - 2 * (row % 2)).astype(jnp.float32))
        for c in range(2):
            for d in range(2):
                part = lax.dot_general(
                    same,
                    table[0, d * HALF : d * HALF + HALF, c * HALF : c * HALF + HALF],
                    NT,
                    preferred_element_type=jnp.float32,
                )
                inverse[c * HALF : c * HALF + HALF, d * HALF : d * HALF + HALF] = (
                    part * factor
                ).astype(jnp.bfloat16)

    def turn_sources(window_group):
        order = zero_one(row % 16 // 2 * 32 + row % 32 // 16 * 16 + row % 2 * 8 + row // 32 == column)
        same = zero_one(row == column)
        low_lane = lax.broadcasted_iota(jnp.int32, (HALF, 128), 1) < 64
        zero_row = lax.broadcasted_iota(jnp.int32, (HALF, 128), 0) == 0
        for g in range(2):
            block = panels[pl.ds(window_group * 4 + g * 2, 2)].reshape(256, WIN)
            rows = jnp.dot(order, block, preferred_element_type=jnp.float32).astype(jnp.bfloat16)
            for w in range(8):
                for b in range(2):
                    for copy in range(2):
                        start = w * 128 + copy * 64 + b * 32 + g * 16
                        turned[start : start + 16, :] = rows[w * 32 + b * 16 : w * 32 + b * 16 + 16]
        for n in range(4):
            real, imag = (
                lax.dot_general(
                    same,
                    turned[n * 256 : n * 256 + 256, c * HALF : c * HALF + HALF],
                    NT,
                    preferred_element_type=jnp.float32,
                )
                for c in range(2)
            )
            for w in range(2):
                re, im = real[:, w * 128 : w * 128 + 128], imag[:, w * 128 : w * 128 + 128]
                window = window_group * 8 + n * 2 + w
                sources[pl.ds(window, HALF, stride=STEP), :] = jnp.where(
                    low_lane, re, jnp.where(zero_row, 0.0, -im)
                )
                sources[pl.ds(32 + window, HALF, stride=STEP), :] = jnp.where(
                    low_lane, jnp.where(zero_row, 0.0, im), jnp.where(zero_row, im, re)
                )

    barrier = pltpu.get_barrier_semaphore()

    @pl.when(y != seg)
    def _():
        pl.semaphore_signal(barrier, inc=1, device_id=((seg * 4 + x) * 4 + zh, y), device_id_type=MESH)

    @pl.loop(1, 16)
    def _(step):
        pl.semaphore_signal(barrier, inc=1, device_id=(plane_peer(step) * 4 + zh, seg), device_id_type=MESH)

    @pl.loop(1, 8)
    def _(step):
        z = (zh * 2 + zl + step) % 8
        pl.semaphore_signal(
            barrier, inc=1, device_id=(plane * 4 + z // 2, (z % 2) * 2 + core), device_id_type=MESH
        )

    pl.semaphore_signal(barrier, inc=1, device_id=(recv, zl * 2 + 1 - core), device_id_type=MESH)
    prepare(zh, blocks, raw, owner, table, slots, first, spectra)
    kept_chunk = pltpu.make_async_copy(first, chunk, local_sem.at[6])
    own_chunk = pltpu.make_async_copy(chunk, panels.at[plane, zh], local_sem.at[4])

    @pl.when(y == seg)
    def _():
        kept_chunk.start()

    own = pltpu.make_async_copy(slots.at[plane], staged.at[:, plane], local_sem.at[0])
    own.start()

    @pl.when(y == seg)
    def _():
        pl.semaphore_wait(barrier, 23)

    @pl.when(y != seg)
    def _():
        pl.semaphore_wait(barrier, 24)
        turn_copy().start()

    for group in range(len(GROUPS)):

        @pl.loop(1, 16)
        def _(step):
            xy_copy(group, step).start()

    @pl.when(y != seg)
    def _():
        turn_copy().wait()

    @pl.when(y == seg)
    def _():
        kept_chunk.wait()

    own_chunk.start()
    for turn in (1, 2, 3):
        pz_copy(turn).start()

    kept = pltpu.make_async_copy(staged.at[ORDER.index(0)], held.at[seg, :, zh], local_sem.at[5])
    own.wait()
    for group, (start, count) in enumerate(GROUPS):

        @pl.loop(1, 16)
        def _(step):
            xy_copy(group, step).wait_recv()

        for turn in ORDER[start : start + count]:
            for half in range(2):
                z_copy(turn, near[turn] if turn else 1 - zl, half).start()
            if not turn:
                kept.start()
        if group == 0:
            own_chunk.wait()
            for other in (1, 2, 3):
                pz_copy(other).wait_recv()

            @pl.loop(1, 16)
            def _(step):
                pxy_copy(step).start()

    kept.wait()
    for half in range(2):
        core_copy(0, zl, half).start()
    direct, far = 1 + 2 * zl, 3 - 2 * zl
    for turn, low in ((2, 1 - zl), (direct, 0), (direct, 1)):
        for half in range(2):
            z_arrival(turn, low, half).wait_recv()
            pair_copy(turn, low, half).start()
            core_copy(turn, low, half).start()
    for half in range(2):
        z_arrival(0, 1 - zl, half).wait_recv()
        core_copy(0, 1 - zl, half).start()

    early = ((0, zl), (2, 1 - zl), (direct, 0), (direct, 1), (0, 1 - zl))
    late = ((2, zl), (far, 0), (far, 1))
    for turn, low in early:
        place_block(low * 2 + core, (zh + 4 - turn) % 4)
    for turn, low in early:
        for half in range(2):
            core_arrival(turn, low, half).wait_recv()
        place_block(low * 2 + 1 - core, (zh + 4 - turn) % 4)

    turn_table()

    @pl.loop(1, 16)
    def _(step):
        pxy_copy(step).wait_recv()

    @pl.loop(0, 4)
    def _(window_group):
        turn_sources(window_group)

    for turn, low in late:
        for half in range(2):
            pair_copy(turn, low, half).wait_recv()
            core_copy(turn, low, half).start()
        place_block(low * 2 + core, (zh + 4 - turn) % 4)
    for turn, low in late:
        for half in range(2):
            core_arrival(turn, low, half).wait_recv()
        place_block(low * 2 + 1 - core, (zh + 4 - turn) % 4)
    turn_receivers()

    @pl.loop(1, 16)
    def _(step):
        pxy_copy(step).wait_send()
        for group in range(len(GROUPS)):
            xy_copy(group, step).wait_send()

    for turn in (1, 2, 3):
        pz_copy(turn).wait_send()
    for half in range(2):
        for turn in range(4):
            z_copy(turn, near[turn] if turn else 1 - zl, half).wait_send()
            for low in (0, 1):
                core_copy(turn, low, half).wait_send()
        for turn, low in ((2, 1 - zl), (direct, 0), (direct, 1)):
            pair_copy(turn, low, half).wait_send()


def exchange(raw_data, row_owner, source_blocks):
    dma = pltpu.SemaphoreType.DMA
    bf16 = jnp.bfloat16
    return pl.pallas_call(
        exchange_kernel,
        out_shape=(
            jax.ShapeDtypeStruct((HALF * STEP, 128), jnp.float32),
            jax.ShapeDtypeStruct((HALF * STEP, 128), jnp.float32),
            jax.ShapeDtypeStruct((WIN, WIN), jnp.bfloat16),
        ),
        in_specs=[pl.BlockSpec(memory_space=pltpu.SMEM)] + [pl.BlockSpec(memory_space=pltpu.VMEM)] * 3,
        out_specs=(pl.BlockSpec(memory_space=pltpu.VMEM),) * 3,
        scratch_shapes=[
            pltpu.VMEM((512, WIN), bf16),
            pltpu.VMEM((16, 4, 16, WIN), bf16),
            pltpu.VMEM((32, WIN), bf16),
            pltpu.VMEM((4, 16, 4, 16, WIN), bf16),
            pltpu.VMEM((16, 4, 32, WIN), bf16),
            pltpu.VMEM((4096, WIN), bf16),
            pltpu.VMEM((1024, WIN), bf16),
            pltpu.VMEM((4, 16, 16, WIN), bf16),
            pltpu.VMEM((32, WIN), bf16),
            dma, dma, dma((4, 16)), dma((4, 16)), dma((4, 2)), dma((4, 2, 2)),
            dma((4, 2, 2)), dma((4, 2, 2)), dma((4, 2, 2)), dma((4, 2, 2)),
            dma((4,)), dma((4,)), dma((16,)), dma((16,)), dma((7,)),
        ],
        compiler_params=pltpu.CompilerParams(
            collective_id=0, has_side_effects=True, vmem_limit_bytes=24576 * 1024
        ),
        name="exchange",
    )(source_blocks, raw_data, row_owner.reshape(1, 64), forward_halves())


def correlate_kernel(sources, receivers, inverse, out, stack, lagged, sent):
    @pl.loop(0, HALF, unroll=64)
    def _(j):
        at = pl.ds(pl.multiple_of(j * STEP, 8), 64)
        terms = lax.dot_general(
            sources[at, :].astype(jnp.bfloat16),
            receivers[at, :].astype(jnp.bfloat16),
            TN,
            preferred_element_type=jnp.float32,
        )
        stack[pl.ds(j, 64, stride=PITCH), :] = terms[:64]
        stack[pl.ds(HALF + j, 64, stride=PITCH), :] = terms[64:]

    def out_copy(group, slot):
        return pltpu.make_async_copy(lagged.at[slot], out.at[pl.ds(group * 8, 8)], sent.at[slot])

    @pl.loop(0, 4)
    def _(pair):
        for slot in range(2):
            group = pair * 2 + slot

            @pl.when(pair > 0)
            def _():
                out_copy(group - 2, slot).wait()

            @pl.loop(0, 8, unroll=8)
            def _(i):
                start = (group * 8 + i) * PITCH
                lagged[slot, i] = lax.dot_general(
                    stack[pl.ds(pl.multiple_of(start, 8), WIN), :].astype(jnp.bfloat16),
                    inverse[...],
                    TN,
                    preferred_element_type=jnp.float32,
                ).astype(jnp.bfloat16)

            out_copy(group, slot).start()

    for slot in range(2):
        out_copy(6 + slot, slot).wait()


def correlate(sources, receivers, inverse):
    return pl.pallas_call(
        correlate_kernel,
        out_shape=jax.ShapeDtypeStruct((64, 128, WIN), jnp.bfloat16),
        in_specs=[pl.BlockSpec(memory_space=pltpu.VMEM)] * 3,
        out_specs=pl.BlockSpec(memory_space=pl.ANY),
        scratch_shapes=[
            pltpu.VMEM((64 * PITCH, 128), jnp.float32),
            pltpu.VMEM((2, 8, 128, WIN), jnp.bfloat16),
            pltpu.SemaphoreType.DMA((2,)),
        ],
        compiler_params=pltpu.CompilerParams(vmem_limit_bytes=24 * 1024 * 1024),
        name="correlate",
    )(sources, receivers, inverse)


def local(raw_data, row_owner, source_blocks):
    sources, receivers, inverse = exchange(raw_data, row_owner, source_blocks)
    lagged = correlate(sources, receivers, inverse)
    return lagged.reshape(2, 32, 128, WIN)


def solution(mesh):
    placed = (P("seg", "recv", None), P("recv", None), P())
    return jax.shard_map(
        local, mesh=mesh, in_specs=placed, out_specs=P(None, "seg", "recv", None), check_vma=False
    )
```
